32 devices in a mesh: dp: 4 (over x, core), expert: 8 (over z, y).
Axes of the slice: x: 2, y: 2, z: 4, core: 2. Of those that a mesh axis runs over, the one named last changes fastest.
Arguments:
- tokens: bfloat16 [8192, 768], P(('dp', 'expert')), may hold values from -6 to 6
- upstream: bfloat16 [8192, 768], P(('dp', 'expert')), may hold values from -4 to 4
- gate_prob: float32 [8192], P(('dp', 'expert')), may hold values from 0.2 to 1
- expert_id: int32 [8192], P(('dp', 'expert')), may hold values from 0 to 7
- slot_index: int32 [8192], P(('dp', 'expert')), may hold values from -1 to 39, as said below
- segment_id: int32 [32, 256], P(('dp', 'expert')), may hold values from 0 to 3, never falling along the last dimension, each value on 1 to 128 neighbouring positions
- weight_in: bfloat16 [8, 3072, 768], P('expert'), may hold values from -0.21875 to 0.21875
- weight_out: bfloat16 [8, 3072, 768], P('expert'), may hold values from -0.109375 to 0.109375
Outputs:
- d_tokens: bfloat16 [8192, 768], P(('dp', 'expert'))
- d_gate: float32 [8192], P(('dp', 'expert'))
- grad_in: bfloat16 [8, 3072, 768], P('expert', 'dp')
- grad_out: bfloat16 [8, 3072, 768], P('expert', 'dp')
The draws below stay inside these ranges and needn't reach their ends.
Inputs may be any that keep to these rules, and one draw needn't show every extreme that they name: `slot_index`: -1 marks a dropped token; otherwise the number of earlier tokens of the same row with the same expert_id. A token is dropped exactly when 40 or more earlier tokens of its row chose its expert. `segment_id`: never falling along a row.
All inputs are finite; a program needn't handle non-finite values.
Results may differ from the reference program's by a relative error of at most 0.02.
Values may be sent and summed in bfloat16 or wider, within the bound.
No kernel may reach another device: no remote copies, remote signals or barrier semaphores. Data moves between devices by JAX's collectives and lax.ppermute only.
A program may use at most 128 MiB of HBM per device.

```python
import math
from functools import partial
import jax
import jax.numpy as jnp
import numpy as np
from jax import lax

D = 768
FF = 3072
TOK_DEV = 256
SEGS = 4
EXPERTS = 8
CAP = 40
MOST_SEG = 128
TOKENS = 8192
N_DP = 4
N_EXPERT = 8


def routing_pair(key):
    devices = TOKENS // TOK_DEV
    favored = jax.random.randint(jax.random.fold_in(key, 11), (), 0, EXPERTS)
    spread = jax.random.randint(jax.random.fold_in(key, 12), (devices, TOK_DEV), 0, EXPERTS)
    scores = jax.random.randint(jax.random.fold_in(key, 13), (devices, TOK_DEV), 0, 4096) * TOK_DEV
    scores = scores + jnp.arange(TOK_DEV, dtype=jnp.int32)[None, :]
    order = jnp.argsort(scores, axis=1)
    ranks = jnp.argsort(order, axis=1)
    chosen = jnp.where(ranks < CAP + 1, favored, spread).astype(jnp.int32)
    member = (chosen[:, :, None] == jnp.arange(EXPERTS, dtype=jnp.int32)[None, None, :]).astype(jnp.int32)
    before = jnp.cumsum(member, axis=1) - member
    places = jnp.sum(before * member, axis=2)
    places = jnp.where(places < CAP, places, -1).astype(jnp.int32)
    return (chosen.reshape(TOKENS), places.reshape(TOKENS))


def draw_expert_id(key, part):
    chosen, places = routing_pair(key)
    return chosen


def draw_slot_index(key, part):
    chosen, places = routing_pair(key)
    return places


def block_levels(own_key, shape, pieces, low, top_value):
    gain, own = 1.0, jax.random.fold_in(own_key, 6)
    for dim, blocks in pieces:
        steps = jnp.exp(jax.random.uniform(jax.random.fold_in(own, dim), (blocks,), jnp.float32, low / len(pieces), top_value / len(pieces)))
        gain = gain * jnp.repeat(steps, shape[dim] // blocks).reshape([-1 if axis == dim else 1 for axis in range(len(shape))])
    return gain


def profile(amount, total, most, skew):
    weights = [(1 << 20) // math.isqrt(grade ** skew) + 1 for grade in range(2, amount + 1)]
    rest, holding = total - most - (amount - 1), [1] * (amount - 1)
    while rest > 0:
        candidates = [i for i in range(amount - 1) if holding[i] < most]
        pool, remaining = sum([weights[i] for i in candidates]), rest
        for i in candidates:
            addition = min(most - holding[i], max(1, remaining * weights[i] // pool), rest)
            holding[i] = holding[i] + addition
            rest = rest - addition
    return np.array([most] + holding)


def uneven_parts(key, number_of, total, most, lean):
    if number_of == 2:
        one = jax.random.randint(key, (), max(1, total - most), min(most, total - 1) + 1)
        return jnp.stack([one, total - one])
    tallies = jnp.asarray(profile(number_of, total, most, lean), jnp.int32)
    twos = (number_of - 1) // 2
    source_of, receiver = tallies[1:1 + 2 * twos:2], tallies[2:2 + 2 * twos:2]
    room = jnp.minimum(source_of - 1, most - receiver)
    moved = jax.random.randint(jax.random.fold_in(key, 1), (twos,), 0, 1 << 20) % (room + 1)
    tallies = tallies.at[1:1 + 2 * twos:2].set(source_of - moved).at[2:2 + 2 * twos:2].set(receiver + moved)
    return tallies[jax.random.permutation(jax.random.fold_in(key, 2), number_of)]


def centred(key, extent, scale, reach, split=(), held_as=jnp.bfloat16):
    gain = block_levels(key, extent, split, -0.22, 0.18) if split else 1.0
    array = jax.random.normal(key, extent, jnp.float32) * scale * gain
    return jnp.minimum(jnp.maximum(array, -reach), reach).astype(held_as)


def setup_inputs(seed: int = 0) -> dict:
    key_list = jax.random.split(jax.random.key(seed), 9)
    tokens = centred(key_list[0], (TOKENS, D), 1.0, 6.0, ((0, 32),))
    upstream = centred(key_list[1], (TOKENS, D), 0.3, 4.0, ((0, 32),))
    gate_prob = jnp.clip(0.2 + 0.8 * jax.random.uniform(key_list[2], (TOKENS,), jnp.float32) ** block_levels(key_list[2], (TOKENS,), ((0, 32),), -0.2, 0.2), 0.2, 1.0)
    expert_id = draw_expert_id(jax.random.fold_in(key_list[8], 71), 0)
    slot_index = draw_slot_index(jax.random.fold_in(key_list[8], 71), 0)
    segment_id = jax.vmap(lambda own: jnp.searchsorted(jnp.cumsum(uneven_parts(own, SEGS, TOK_DEV, MOST_SEG, 2)), jnp.arange(TOK_DEV), side="right"))(jax.random.split(key_list[5], (N_DP * N_EXPERT))).reshape((N_DP * N_EXPERT, TOK_DEV)).astype(jnp.int32)
    weight_in = centred(key_list[6], (EXPERTS, FF, D), D ** -0.5, 0.21875, ((0, 8),))
    weight_out = centred(key_list[7], (EXPERTS, FF, D), FF ** -0.5, 0.109375, ((0, 8),))
    return dict(tokens=tokens, upstream=upstream, gate_prob=gate_prob, expert_id=expert_id, slot_index=slot_index, segment_id=segment_id, weight_in=weight_in, weight_out=weight_out)


def gelu_back(pre_act, grad_rows):
    return jax.vjp(partial(jax.nn.gelu, approximate=True), pre_act)[1](grad_rows)[0]

def pick_rows(values, owners):
    padding = jnp.zeros((1,) + values.shape[1:], values.dtype)
    return jnp.concatenate([values, padding], axis=0)[owners]

def reference(tokens, upstream, gate_prob, expert_id, slot_index, segment_id, weight_in, weight_out):
    groups = N_DP
    sources = N_EXPERT
    devices = groups * sources
    slots_all = EXPERTS * CAP
    highest = lax.Precision.HIGHEST
    labels = jnp.arange(SEGS, dtype=jnp.int32)
    member = (segment_id[:, :, None] == labels[None, None, :]).astype(jnp.float32)
    counts = lax.optimization_barrier(jnp.sum(member, axis=1))
    length = lax.optimization_barrier(jnp.sum(member * counts[:, None, :], axis=2))
    doc_weight = TOK_DEV / (SEGS * length)
    upstream_rows = upstream.reshape(devices, TOK_DEV, D).astype(jnp.float32)
    cotangent = (upstream_rows * doc_weight[:, :, None]).astype(jnp.bfloat16)
    token_rows = tokens.reshape(devices, TOK_DEV, D)
    gate_rows = gate_prob.reshape(devices, TOK_DEV)
    route_rows = expert_id.reshape(devices, TOK_DEV)
    place_rows = slot_index.reshape(devices, TOK_DEV)
    position = jnp.where(place_rows >= 0, route_rows * CAP + place_rows, slots_all).astype(jnp.int32)

    def find_owners(place):
        filled = jnp.full((slots_all + 1,), TOK_DEV, jnp.int32)
        return filled.at[place].set(jnp.arange(TOK_DEV, dtype=jnp.int32))[:slots_all]
    owners = jax.vmap(find_owners)(position)

    def arrange(values):
        sent = jax.vmap(pick_rows)(values, owners)
        sent = sent.reshape((groups, sources, EXPERTS, CAP) + values.shape[2:])
        return jnp.moveaxis(sent, 2, 0)
    x_rows = arrange(token_rows)
    c_rows = arrange(cotangent)
    g_rows = arrange(gate_rows)

    def per_expert(operands):
        x_part, c_part, g_part, w_first, w_second = operands
        x_float = x_part.astype(jnp.float32)
        c_float = c_part.astype(jnp.float32)
        first_float = w_first.astype(jnp.float32)
        second_float = w_second.astype(jnp.float32)
        pre_act = jnp.einsum('gskd,fd->gskf', x_float, first_float, precision=highest)
        hidden = jax.nn.gelu(pre_act, approximate=True).astype(jnp.bfloat16)
        hidden_float = hidden.astype(jnp.float32)
        produced = jnp.einsum('gskf,fd->gskd', hidden_float, second_float, precision=highest)
        d_gate_rows = lax.optimization_barrier(jnp.sum(produced * c_float, axis=3))
        d_out = (g_part[..., None] * c_float).astype(jnp.bfloat16)
        d_out_float = d_out.astype(jnp.float32)
        d_hidden = jnp.einsum('gskd,fd->gskf', d_out_float, second_float, precision=highest)
        d_pre = gelu_back(pre_act, d_hidden).astype(jnp.bfloat16)
        d_pre_float = d_pre.astype(jnp.float32)
        d_in_rows = jnp.einsum('gskf,fd->gskd', d_pre_float, first_float, precision=highest).astype(jnp.bfloat16)
        grad_second = jnp.einsum('gskf,gskd->fd', hidden_float, d_out_float, precision=highest).astype(jnp.bfloat16)
        grad_first = jnp.einsum('gskf,gskd->fd', d_pre_float, x_float, precision=highest).astype(jnp.bfloat16)
        return (d_in_rows, d_gate_rows, grad_first, grad_second)
    d_in_rows, d_gate_rows, grad_in, grad_out = lax.map(per_expert, (x_rows, c_rows, g_rows, weight_in, weight_out))

    def send_back(values):
        moved = jnp.moveaxis(values, 0, 2).reshape((devices, slots_all) + values.shape[4:])
        return jax.vmap(pick_rows)(moved, position)
    d_tokens = send_back(d_in_rows).reshape(TOKENS, D)
    d_gate = send_back(d_gate_rows).reshape(TOKENS)
    return (d_tokens, d_gate, grad_in, grad_out)
```

```python
from functools import partial

import jax
import jax.numpy as jnp
from jax import lax
from jax.experimental import pallas as pl
from jax.experimental.pallas import tpu as pltpu
from jax.sharding import PartitionSpec as P

SEGS = 4
LANES = 128
SUBLANES = 8
MIB = 1024 * 1024
ROOT_2_PI = 0.7978845608028654
CUBIC = 0.044715


def dot_nn(a, b):
    return lax.dot_general(a, b, (((1,), (0,)), ((), ())), preferred_element_type=jnp.float32)


def dot_nt(a, b):
    return lax.dot_general(a, b, (((1,), (1,)), ((), ())), preferred_element_type=jnp.float32)


def dot_tn(a, b):
    return lax.dot_general(a, b, (((0,), (0,)), ((), ())), preferred_element_type=jnp.float32)


def gelu_and_slope(v):
    square = v * v
    t = jnp.tanh(v * (ROOT_2_PI + (ROOT_2_PI * CUBIC) * square))
    half = 0.5 + 0.5 * t
    hidden = v * half
    slope = half + hidden * (1.0 - t) * (ROOT_2_PI + (3.0 * ROOT_2_PI * CUBIC) * square)
    return hidden.astype(jnp.bfloat16), slope


def owner_table(chunk, slot, cap_rows, slots):
    place = jnp.where(slot >= 0, chunk * cap_rows + slot, -1)
    rows = lax.broadcasted_iota(jnp.int32, (slots, slot.shape[1]), 0)
    return rows == place


def pack_kernel(cap_rows, experts, me_ref, *refs):
    pairs = experts // 2
    sources, x_refs, (keep_ref, cross_ref) = refs[:6], refs[6 : 6 + pairs], refs[6 + pairs : 8 + pairs]
    scratch, sems = refs[8 + pairs : 14 + pairs], refs[14 + pairs]
    copies = [
        pltpu.make_async_copy(src, dst, sems.at[i])
        for i, (src, dst) in enumerate(zip(sources, scratch))
    ]
    for copy in copies:
        copy.start()
    for copy in copies:
        copy.wait()
    tok_ref, up_ref, gate_ref, expert_ref, slot_ref, seg_ref = scratch
    tok_rows = tok_ref.shape[0]
    slots = experts * cap_rows
    chunk, slot = expert_ref[...] ^ me_ref[0], slot_ref[...]
    table = owner_table(chunk, slot, cap_rows, slots).astype(jnp.bfloat16)
    split_rows(dot_nn(table, tok_ref[...]), x_refs)
    seg = seg_ref[...]
    length = jnp.zeros(seg.shape, jnp.float32)
    for label in range(SEGS):
        member = (seg == label).astype(jnp.float32)
        length = length + member * jnp.sum(member, axis=1, keepdims=True)
    weight = tok_rows / (SEGS * length)
    chosen = owner_table((chunk & 1) * pairs + (chunk >> 1), slot, cap_rows, slots)
    table = chosen.astype(jnp.bfloat16)
    weight_col = jnp.sum(jnp.where(chosen, weight, 0.0), axis=1, keepdims=True)
    gate_col = jnp.sum(jnp.where(chosen, gate_ref[...], 0.0), axis=1, keepdims=True)
    cotangent = (dot_nn(table, up_ref[...]) * weight_col).astype(jnp.bfloat16)
    split_rows(cotangent.astype(jnp.float32) * gate_col, (keep_ref, cross_ref))


def split_rows(value, refs):
    rows = value.shape[0] // len(refs)
    for i, ref in enumerate(refs):
        ref[...] = value[i * rows : (i + 1) * rows].astype(ref.dtype)


def halves(refs):
    values = [ref[...].astype(jnp.float32) for ref in refs]
    half = values[0].shape[0] // 2
    return [jnp.concatenate([v[b * half : (b + 1) * half] for v in values], axis=0) for b in (0, 1)]


def turn_d_kernel(pairs, keep_ref, near_ref, *out_refs):
    both = [ref[...].astype(jnp.float32) for ref in (keep_ref, near_ref)]
    rows = both[0].shape[0] // pairs
    for i, ref in enumerate(out_refs):
        ref[...] = jnp.concatenate([v[i * rows : (i + 1) * rows] for v in both], axis=0).astype(ref.dtype)


def turn_x_kernel(after_ref, *refs):
    for ref, value in zip(refs[-2:], halves(refs[:-2])):
        ref[...] = value.astype(ref.dtype)


def join_kernel(after_ref, x_ref, *refs):
    refs, (d_ref, own_ref) = refs[:-2], refs[-2:]
    rows = x_ref.shape[0]
    value = jnp.concatenate(halves(refs), axis=0).astype(d_ref.dtype)
    d_ref[...] = value
    own_ref[:rows, :] = x_ref[...]
    own_ref[rows:, :] = value


def copy_share(which_ref, source, target, sem):
    share = target.shape[0]
    start = pl.multiple_of(which_ref[0] * share, share)
    return pltpu.make_async_copy(source.at[pl.ds(start, share), :], target, sem)


def forward_kernel(after_ref, x_ref, d_ref, out_ref):
    gather_rows((x_ref, d_ref), out_ref)


def tile_copies(pairs, sems, i, tile):
    here = block(i, tile)
    return [
        pltpu.make_async_copy(source.at[here, :], target.at[here, :], sems.at[i, k])
        for k, (source, target) in enumerate(pairs)
    ]


def over_tiles(pairs, sems, steps, tile, work):
    def start(i):
        for copy in tile_copies(pairs, sems, i, tile):
            copy.start()

    start(0)
    start(1)

    def step(i, carry):
        @pl.when(i + 2 < steps)
        def _():
            start(i + 2)

        for copy in tile_copies(pairs, sems, i, tile):
            copy.wait()
        work(i)
        return carry

    lax.fori_loop(0, steps, step, 0)


def own_first_kernel(rows_ref, first_src, hidden_ref, slope_ref, first_ref, sems):
    steps, tile = hidden_ref.shape[0], hidden_ref.shape[2]

    def work(i):
        hidden, slope = gelu_and_slope(dot_nt(rows_ref[...], first_ref[block(i, tile), :]))
        hidden_ref[i] = hidden
        slope_ref[i] = slope.astype(slope_ref.dtype)

    over_tiles([(first_src, first_ref)], sems, steps, tile, work)


def own_second_kernel(
    rows_ref,
    hidden_ref,
    slope_ref,
    first_src,
    second_src,
    total_ref,
    gate_ref,
    first_ref,
    second_ref,
    sems,
):
    steps, tile = hidden_ref.shape[0], hidden_ref.shape[2]
    total_ref[...] = jnp.zeros_like(total_ref)
    gate_ref[...] = jnp.zeros_like(gate_ref)

    def work(j):
        here = block(j, tile)
        back = dot_nt(rows_ref[...], second_ref[here, :])
        terms = hidden_ref[j].astype(jnp.float32) * back
        gate = gate_ref[...]
        for i in range(tile // LANES):
            gate = gate + terms[:, i * LANES : (i + 1) * LANES]
        gate_ref[...] = gate
        d_pre = (back * slope_ref[j].astype(jnp.float32)).astype(jnp.bfloat16)
        total_ref[...] += dot_nn(d_pre, first_ref[here, :])

    over_tiles([(second_src, second_ref), (first_src, first_ref)], sems, steps, tile, work)


def chunks_kernel(cap_rows, me_ref, x_over, core, total_ref, gate_ref, out_ref):
    experts = out_ref.shape[0]
    total = total_ref[...]
    gates = jnp.sum(gate_ref[...], axis=1, keepdims=True)
    lane = lax.broadcasted_iota(jnp.int32, (SUBLANES, LANES), 1)
    for k in range(experts):
        start = k * cap_rows
        tail = jnp.zeros((SUBLANES, LANES), jnp.float32)
        for i in range(cap_rows // SUBLANES):
            here = start + i * SUBLANES
            tail = jnp.where(lane == i, gates[here : here + SUBLANES], tail)
        parts = [
            total[start : start + cap_rows, i * LANES : (i + 1) * LANES]
            for i in range(total.shape[1] // LANES)
        ]
        source = me_ref[0] ^ (2 * (k % (experts // 2)) + k // (experts // 2))
        out_ref[source] = jnp.concatenate(parts + [tail], axis=0).astype(out_ref.dtype)


def gather_rows(refs, all_ref):
    rows = refs[0].shape[0]
    for i, ref in enumerate(refs):
        all_ref[i * rows : (i + 1) * rows, :] = ref[...]


def block(i, tile=256):
    return pl.ds(pl.multiple_of(i * tile, tile), tile)


def gelu_rows(weights_ref, rows_ref, hidden_ref, slope_ref):
    tile = weights_ref.shape[0] // 2

    def step(i, carry):
        here = block(i, tile)
        hidden, slope = gelu_and_slope(dot_nt(weights_ref[here, :], rows_ref[...]))
        hidden_ref[here, :] = hidden
        slope_ref[here, :] = slope.astype(slope_ref.dtype)
        return carry

    lax.fori_loop(0, 2, step, 0)


def weight_terms(weights_ref, x_ref, d_ref, hidden_ref, slope_ref, finish):
    tile = weights_ref.shape[0] // 2

    def step(i, carry):
        here = block(i, tile)
        back = dot_nt(weights_ref[here, :], d_ref[...])
        d_pre = (back * slope_ref[here, :].astype(jnp.float32)).astype(jnp.bfloat16)
        finish(i, here, dot_nn(d_pre, x_ref[...]), dot_nn(hidden_ref[here, :], d_ref[...]))
        return carry

    lax.fori_loop(0, 2, step, 0)


def near_first_kernel(
    which_ref,
    after_ref,
    a_ref,
    b_ref,
    first_src,
    second_src,
    hidden_ref,
    slope_ref,
    all_ref,
    first_ref,
    second_ref,
    sems,
):
    first_copy = copy_share(which_ref, first_src, first_ref, sems.at[0])
    second_copy = copy_share(which_ref, second_src, second_ref, sems.at[1])
    first_copy.start()
    second_copy.start()
    rows = a_ref.shape[0] // 2
    gather_rows((a_ref.at[:rows], b_ref.at[:rows]), all_ref)
    first_copy.wait()
    gelu_rows(first_ref, all_ref, hidden_ref, slope_ref)
    second_copy.wait()


def near_second_kernel(
    after_ref, a_ref, b_ref, x_ref, hidden_ref, slope_ref, second_ref, gin_ref, gout_ref, all_ref
):
    rows = a_ref.shape[0] // 2
    gather_rows((a_ref.at[rows:], b_ref.at[rows:]), all_ref)

    def finish(i, here, gin, gout):
        gin_ref[here, :] = gin
        gout_ref[here, :] = gout

    weight_terms(second_ref, x_ref, all_ref, hidden_ref, slope_ref, finish)


def far_first_kernel(after_ref, x_over, diagonal_ref, first_ref, hidden_ref, slope_ref, x_ref):
    gather_rows((x_over, diagonal_ref.at[: x_over.shape[0]]), x_ref)
    gelu_rows(first_ref, x_ref, hidden_ref, slope_ref)


def far_second_kernel(
    after_ref,
    d_over,
    diagonal_ref,
    x_ref,
    hidden_ref,
    slope_ref,
    second_ref,
    gin_near,
    gout_near,
    gin_out,
    gout_out,
    d_ref,
    gin_ref,
    gout_ref,
    sems,
):
    gather_rows((d_over, diagonal_ref.at[d_over.shape[0] :]), d_ref)
    tile = second_ref.shape[0] // 2

    def copies(i):
        here = block(i, tile)
        return [
            pltpu.make_async_copy(gin_ref.at[here, :], gin_out.at[here, :], sems.at[i, 0]),
            pltpu.make_async_copy(gout_ref.at[here, :], gout_out.at[here, :], sems.at[i, 1]),
        ]

    def finish(i, here, gin, gout):
        gin_ref[here, :] = (gin_near[here, :] + gin).astype(gin_ref.dtype)
        gout_ref[here, :] = (gout_near[here, :] + gout).astype(gout_ref.dtype)
        for copy in copies(i):
            copy.start()

    weight_terms(second_ref, x_ref, d_ref, hidden_ref, slope_ref, finish)
    for i in range(2):
        for copy in copies(i):
            copy.wait()


def unpack_kernel(
    cap_rows, after_ref, back_ref, gate_ref, expert_ref, slot_ref, tok_ref, dgate_ref
):
    experts = back_ref.shape[0]
    blocks = tok_ref.shape[1] // LANES
    lane = lax.broadcasted_iota(jnp.int32, (SUBLANES, LANES), 1)
    rows, gates = [], []
    for e in range(experts):
        value = back_ref[e].astype(jnp.float32)
        pieces = [value[i * cap_rows : (i + 1) * cap_rows] for i in range(blocks)]
        rows.append(jnp.concatenate(pieces, axis=1))
        tail = value[cap_rows * blocks :]
        gates += [jnp.where(lane == i, tail, 0.0) for i in range(cap_rows // SUBLANES)]
    rows = jnp.concatenate(rows, axis=0).astype(jnp.bfloat16)
    gates = jnp.concatenate(gates, axis=0).astype(jnp.bfloat16)
    chosen = owner_table(expert_ref[...], slot_ref[...], cap_rows, experts * cap_rows)
    table = chosen.astype(jnp.bfloat16)
    tok_ref[...] = dot_tn(table, rows).astype(jnp.bfloat16)
    picked = jnp.sum(dot_tn(gates, table), axis=0, keepdims=True)
    dgate_ref[...] = picked / gate_ref[...]


def in_hbm(*arrays):
    return [pltpu.with_memory_space_constraint(a, pltpu.HBM) for a in arrays]


def body(tokens, upstream, gate_prob, expert_id, slot_index, segment_id, weight_in, weight_out):
    experts = lax.axis_size("expert")
    groups = lax.axis_size("dp")
    tok_rows, width = tokens.shape
    hidden_units = weight_in.shape[1]
    capacity = 5 * tok_rows // (4 * experts)
    cap_rows = -(-capacity // SUBLANES) * SUBLANES
    slots = experts * cap_rows
    share = hidden_units // groups
    gate_row = gate_prob.reshape(1, tok_rows)
    expert_row = expert_id.reshape(1, tok_rows)
    slot_row = slot_index.reshape(1, tok_rows)
    pairs = experts // 2
    which = lax.axis_index("dp").astype(jnp.int32).reshape(1)
    me = lax.axis_index("expert").astype(jnp.int32).reshape(1)
    bf16 = jnp.bfloat16
    anywhere = pl.BlockSpec(memory_space=pl.ANY)
    smem = pl.BlockSpec(memory_space=pltpu.SMEM)
    vmem = pl.BlockSpec(memory_space=pltpu.VMEM)

    unit = 2 * slots * width * hidden_units

    def call(kernel, name, ins, outs, scratch=(), out_spec=vmem, limit=10, work=0.0):
        return pl.pallas_call(
            kernel,
            in_specs=ins,
            out_specs=[out_spec] * len(outs),
            out_shape=[jax.ShapeDtypeStruct(shape, dtype) for shape, dtype in outs],
            scratch_shapes=list(scratch),
            compiler_params=pltpu.CompilerParams(vmem_limit_bytes=limit * MIB),
            cost_estimate=pl.CostEstimate(
                flops=int(work * unit), bytes_accessed=int(work * unit) // 512, transcendentals=0
            ),
            name=name,
        )

    def across(chunk, mask):
        return lax.ppermute(chunk, "expert", [(i, i ^ mask) for i in range(experts)])

    def over(chunk, mask):
        return lax.ppermute(chunk, "dp", [(i, i ^ mask) for i in range(groups)])

    row = (1, tok_rows)
    part = ((2 * cap_rows, width), bf16)
    half = ((pairs * cap_rows, width), bf16)
    *x_parts, d_keep, d_cross = call(
        partial(pack_kernel, cap_rows, experts),
        "pack",
        [smem] + [anywhere] * 6,
        [part] * pairs + [half] * 2,
        [
            pltpu.VMEM((tok_rows, width), bf16),
            pltpu.VMEM((tok_rows, width), bf16),
            pltpu.VMEM(row, jnp.float32),
            pltpu.VMEM(row, jnp.int32),
            pltpu.VMEM(row, jnp.int32),
            pltpu.VMEM(row, jnp.int32),
            pltpu.SemaphoreType.DMA((6,)),
        ],
    )(me, *in_hbm(tokens, upstream, gate_row, expert_row, slot_row, segment_id))
    order = list(range(pairs - 1, 0, -1))
    x_near = {s: across(x_parts[s], 2 * s) for s in order}
    x_near = [x_parts[0]] + [x_near[s] for s in range(1, pairs)]
    d_near = across(d_cross, 1)
    d_parts = call(
        partial(turn_d_kernel, pairs),
        "turn_d",
        [vmem] * 2,
        [part] * pairs,
    )(d_keep, d_near)
    x_keep, x_cross = call(
        turn_x_kernel,
        "turn_x",
        [anywhere] + [vmem] * pairs,
        [half] * 2,
    )(d_parts[0], *x_near)
    d_far = {s: across(d_parts[s], 2 * s) for s in order}
    d_far = [d_parts[0]] + [d_far[s] for s in range(1, pairs)]
    x_own = jnp.concatenate([x_keep, across(x_cross, 1)], axis=0)

    wide = ((groups, slots, share), bf16)
    weights = pltpu.VMEM((hidden_units, width), bf16)
    hidden, slope = call(
        own_first_kernel,
        "own_first",
        [vmem, anywhere],
        [wide] * 2,
        [weights, pltpu.SemaphoreType.DMA((groups, 1))],
        limit=20,
        work=1,
    )(x_own, *in_hbm(weight_in[0]))
    pair_rows = ((2 * slots, width), bf16)
    d_own, own = call(
        join_kernel,
        "join",
        [anywhere] + [vmem] * (pairs + 1),
        [((slots, width), bf16), pair_rows],
    )(hidden, x_own, *d_far)
    x_over, d_over, core = over(x_own, 2), over(d_own, 2), over(own, 1)

    stride = cap_rows * width // LANES + SUBLANES
    total, gates = call(
        own_second_kernel,
        "own_second",
        [vmem] * 3 + [anywhere] * 2,
        [((slots, width), jnp.float32), ((slots, LANES), jnp.float32)],
        [weights, weights, pltpu.SemaphoreType.DMA((groups, 2))],
        limit=24,
        work=20,
    )(d_own, hidden, slope, *in_hbm(weight_in[0], weight_out[0]))
    (back,) = call(
        partial(chunks_kernel, cap_rows),
        "chunks",
        [smem] + [anywhere] * 2 + [vmem] * 2,
        [((experts, stride, LANES), bf16)],
    )(me, x_over, core, total, gates)
    returned = lax.all_to_all(back, "expert", split_axis=0, concat_axis=0, tiled=True)

    wide = ((share, 2 * slots), bf16)
    share_rows = ((share, width), bf16)
    term = ((share, width), jnp.float32)
    hidden_t, slope_t, x_near, first_share, second_share = call(
        near_first_kernel,
        "near_first",
        [smem] + [anywhere] + [vmem] * 2 + [anywhere] * 2,
        [wide, wide, pair_rows, share_rows, share_rows],
        [pltpu.SemaphoreType.DMA((2,))],
        work=0.5,
    )(which, back, own, core, *in_hbm(weight_in[0], weight_out[0]))
    gin_near, gout_near = call(
        near_second_kernel,
        "near_second",
        [anywhere] + [vmem] * 6,
        [term, term],
        [pltpu.VMEM(*pair_rows)],
        work=15,
    )(back, own, core, x_near, hidden_t, slope_t, second_share)
    (moved,) = call(
        forward_kernel,
        "forward",
        [anywhere, vmem, vmem],
        [pair_rows],
    )(hidden_t, x_over, d_over)
    diagonal = over(moved, 1)
    hidden_t, slope_t, x_far = call(
        far_first_kernel,
        "far_first",
        [anywhere] + [vmem] * 3,
        [wide, wide, pair_rows],
    )(gin_near, x_over, diagonal, first_share)
    share_block = pltpu.VMEM((share, width), bf16)
    grad_first, grad_second = call(
        far_second_kernel,
        "far_second",
        [anywhere] + [vmem] * 8,
        [share_rows] * 2,
        [pltpu.VMEM(*pair_rows), share_block, share_block, pltpu.SemaphoreType.DMA((2, 2))],
        out_spec=anywhere,
        limit=20,
    )(hidden_t, d_over, diagonal, x_far, hidden_t, slope_t, second_share, gin_near, gout_near)

    d_tokens, d_gate = call(
        partial(unpack_kernel, cap_rows),
        "unpack",
        [anywhere] + [vmem] * 4,
        [((tok_rows, width), bf16), (row, jnp.float32)],
    )(*in_hbm(grad_first), returned, gate_row, expert_row, slot_row)
    return (d_tokens, d_gate.reshape(tok_rows), grad_first[None], grad_second[None])


def solution(mesh):
    in_specs = (
        P(("dp", "expert"), None),
        P(("dp", "expert"), None),
        P(("dp", "expert")),
        P(("dp", "expert")),
        P(("dp", "expert")),
        P(("dp", "expert"), None),
        P("expert", None, None),
        P("expert", None, None),
    )
    out_specs = (
        P(("dp", "expert"), None),
        P(("dp", "expert")),
        P("expert", "dp", None),
        P("expert", "dp", None),
    )
    return jax.shard_map(body, mesh=mesh, in_specs=in_specs, out_specs=out_specs, check_vma=False)
```

```python
from functools import partial

import jax
import jax.numpy as jnp
from jax import lax
from jax.experimental import pallas as pl
from jax.experimental.pallas import tpu as pltpu
from jax.sharding import PartitionSpec as P

SEGS = 4
LANES = 128
SUBLANES = 8
MIB = 1024 * 1024
ROOT_2_PI = 0.7978845608028654
CUBIC = 0.044715


def dot_nn(a, b):
    return lax.dot_general(a, b, (((1,), (0,)), ((), ())), preferred_element_type=jnp.float32)


def dot_nt(a, b):
    return lax.dot_general(a, b, (((1,), (1,)), ((), ())), preferred_element_type=jnp.float32)


def dot_tn(a, b):
    return lax.dot_general(a, b, (((0,), (0,)), ((), ())), preferred_element_type=jnp.float32)


def gelu_and_slope(v):
    square = v * v
    t = jnp.tanh(v * (ROOT_2_PI + (ROOT_2_PI * CUBIC) * square))
    half = 0.5 + 0.5 * t
    hidden = v * half
    slope = half + hidden * (1.0 - t) * (ROOT_2_PI + (3.0 * ROOT_2_PI * CUBIC) * square)
    return hidden.astype(jnp.bfloat16), slope


def owner_table(chunk, slot, cap_rows, slots):
    place = jnp.where(slot >= 0, chunk * cap_rows + slot, -1)
    rows = lax.broadcasted_iota(jnp.int32, (slots, slot.shape[1]), 0)
    return rows == place


def pack_kernel(cap_rows, experts, me_ref, *refs):
    pairs = experts // 2
    sources, x_refs, (keep_ref, cross_ref) = refs[:6], refs[6 : 6 + pairs], refs[6 + pairs : 8 + pairs]
    scratch, sems = refs[8 + pairs : 14 + pairs], refs[14 + pairs]
    copies = [
        pltpu.make_async_copy(src, dst, sems.at[i])
        for i, (src, dst) in enumerate(zip(sources, scratch))
    ]
    for copy in copies:
        copy.start()
    for copy in copies:
        copy.wait()
    tok_ref, up_ref, gate_ref, expert_ref, slot_ref, seg_ref = scratch
    tok_rows = tok_ref.shape[0]
    slots = experts * cap_rows
    chunk, slot = expert_ref[...] ^ me_ref[0], slot_ref[...]
    table = owner_table(chunk, slot, cap_rows, slots).astype(jnp.bfloat16)
    split_rows(dot_nn(table, tok_ref[...]), x_refs)
    seg = seg_ref[...]
    length = jnp.zeros(seg.shape, jnp.float32)
    for label in range(SEGS):
        member = (seg == label).astype(jnp.float32)
        length = length + member * jnp.sum(member, axis=1, keepdims=True)
    weight = tok_rows / (SEGS * length)
    chosen = owner_table((chunk & 1) * pairs + (chunk >> 1), slot, cap_rows, slots)
    table = chosen.astype(jnp.bfloat16)
    weight_col = jnp.sum(jnp.where(chosen, weight, 0.0), axis=1, keepdims=True)
    gate_col = jnp.sum(jnp.where(chosen, gate_ref[...], 0.0), axis=1, keepdims=True)
    cotangent = (dot_nn(table, up_ref[...]) * weight_col).astype(jnp.bfloat16)
    split_rows(cotangent.astype(jnp.float32) * gate_col, (keep_ref, cross_ref))


def split_rows(value, refs):
    rows = value.shape[0] // len(refs)
    for i, ref in enumerate(refs):
        ref[...] = value[i * rows : (i + 1) * rows].astype(ref.dtype)


def halves(refs):
    values = [ref[...].astype(jnp.float32) for ref in refs]
    half = values[0].shape[0] // 2
    return [jnp.concatenate([v[b * half : (b + 1) * half] for v in values], axis=0) for b in (0, 1)]


def turn_d_kernel(pairs, keep_ref, near_ref, *out_refs):
    both = [ref[...].astype(jnp.float32) for ref in (keep_ref, near_ref)]
    rows = both[0].shape[0] // pairs
    for i, ref in enumerate(out_refs):
        ref[...] = jnp.concatenate([v[i * rows : (i + 1) * rows] for v in both], axis=0).astype(ref.dtype)


def turn_x_kernel(after_ref, *refs):
    for ref, value in zip(refs[-2:], halves(refs[:-2])):
        ref[...] = value.astype(ref.dtype)


def join_kernel(after_ref, x_ref, *refs):
    refs, own_ref = refs[:-1], refs[-1]
    rows = x_ref.shape[0]
    own_ref[:rows, :] = x_ref[...]
    own_ref[rows:, :] = jnp.concatenate(halves(refs), axis=0).astype(own_ref.dtype)


def copy_share(which_ref, source, target, sem):
    share = target.shape[0]
    start = pl.multiple_of(which_ref[0] * share, share)
    return pltpu.make_async_copy(source.at[pl.ds(start, share), :], target, sem)


def forward_kernel(after_ref, x_ref, d_ref, out_ref):
    gather_rows((x_ref, d_ref), out_ref)


def tile_copies(pairs, sems, i, tile):
    here = block(i, tile)
    return [
        pltpu.make_async_copy(source.at[here, :], target.at[here, :], sems.at[i, k])
        for k, (source, target) in enumerate(pairs)
    ]


def over_tiles(pairs, sems, steps, tile, work):
    for i in range(steps):
        for copy in tile_copies(pairs, sems, i, tile):
            copy.start()

    def step(i, carry):
        def arrived():
            for copy in tile_copies(pairs, sems, i, tile):
                copy.wait()

        work(i, arrived)
        return carry

    lax.fori_loop(0, steps, step, 0)


def own_first_kernel(rows_ref, first_src, hidden_ref, slope_ref, first_ref, sems):
    steps, tile = hidden_ref.shape[0], hidden_ref.shape[2]

    def work(i, arrived):
        arrived()
        hidden, slope = gelu_and_slope(dot_nt(rows_ref[...], first_ref[block(i, tile), :]))
        hidden_ref[i] = hidden
        slope_ref[i] = slope.astype(slope_ref.dtype)

    over_tiles([(first_src, first_ref)], sems, steps, tile, work)


def own_second_kernel(
    cap_rows,
    me_ref,
    own_ref,
    hidden_ref,
    slope_ref,
    second_ref,
    first_src,
    out_ref,
    total_ref,
    gate_ref,
    held_ref,
    first_ref,
    sems,
    out_sems,
):
    steps, tile = hidden_ref.shape[0], hidden_ref.shape[2]
    rows = total_ref.shape[0]

    def work(j, arrived):
        here = block(j, tile)
        back = dot_nt(own_ref[rows:, :], second_ref[here, :])
        terms = hidden_ref[j].astype(jnp.float32) * back
        gate = gate_ref[...]
        for i in range(tile // LANES):
            gate = gate + terms[:, i * LANES : (i + 1) * LANES]
        gate_ref[...] = gate
        d_pre = (back * slope_ref[j].astype(jnp.float32)).astype(jnp.bfloat16)
        arrived()
        total_ref[...] += dot_nn(d_pre, first_ref[here, :])

    total_ref[...] = jnp.zeros_like(total_ref)
    gate_ref[...] = jnp.zeros_like(gate_ref)
    over_tiles([(first_src, first_ref)], sems, steps, tile, work)

    experts, copies = out_ref.shape[0], []
    gates = jnp.sum(gate_ref[...], axis=1, keepdims=True)
    lane = lax.broadcasted_iota(jnp.int32, (SUBLANES, LANES), 1)
    for k in range(experts):
        start = k * cap_rows
        tail = jnp.zeros((SUBLANES, LANES), jnp.float32)
        for i in range(cap_rows // SUBLANES):
            here = start + i * SUBLANES
            tail = jnp.where(lane == i, gates[here : here + SUBLANES], tail)
        parts = [
            total_ref[start : start + cap_rows, i * LANES : (i + 1) * LANES]
            for i in range(total_ref.shape[1] // LANES)
        ]
        held_ref[k] = jnp.concatenate(parts + [tail], axis=0).astype(held_ref.dtype)
        source = me_ref[0] ^ (2 * (k % (experts // 2)) + k // (experts // 2))
        copies.append(pltpu.make_async_copy(held_ref.at[k], out_ref.at[source], out_sems.at[k]))
        copies[-1].start()
    for copy in copies:
        copy.wait()


def gather_rows(refs, all_ref):
    rows = refs[0].shape[0]
    for i, ref in enumerate(refs):
        all_ref[i * rows : (i + 1) * rows, :] = ref[...]


def block(i, tile=256):
    return pl.ds(pl.multiple_of(i * tile, tile), tile)


def gelu_rows(weights_ref, rows_ref, hidden_ref, slope_ref):
    tile = weights_ref.shape[0] // 2

    def step(i, carry):
        here = block(i, tile)
        hidden, slope = gelu_and_slope(dot_nt(weights_ref[here, :], rows_ref[...]))
        hidden_ref[here, :] = hidden
        slope_ref[here, :] = slope.astype(slope_ref.dtype)
        return carry

    lax.fori_loop(0, 2, step, 0)


def weight_terms(weights_ref, x_ref, d_ref, hidden_ref, slope_ref, finish):
    tile = weights_ref.shape[0] // 2

    def step(i, carry):
        here = block(i, tile)
        back = dot_nt(weights_ref[here, :], d_ref[...])
        d_pre = (back * slope_ref[here, :].astype(jnp.float32)).astype(jnp.bfloat16)
        finish(i, here, dot_nn(d_pre, x_ref[...]), dot_nn(hidden_ref[here, :], d_ref[...]))
        return carry

    lax.fori_loop(0, 2, step, 0)


def near_first_kernel(
    which_ref,
    after_ref,
    a_ref,
    b_ref,
    first_src,
    second_src,
    hidden_ref,
    slope_ref,
    all_ref,
    first_ref,
    second_ref,
    sems,
):
    first_copy = copy_share(which_ref, first_src, first_ref, sems.at[0])
    second_copy = copy_share(which_ref, second_src, second_ref, sems.at[1])
    first_copy.start()
    second_copy.start()
    rows = a_ref.shape[0] // 2
    gather_rows((a_ref.at[:rows], b_ref.at[:rows]), all_ref)
    first_copy.wait()
    gelu_rows(first_ref, all_ref, hidden_ref, slope_ref)
    second_copy.wait()


def near_second_kernel(
    after_ref, a_ref, b_ref, x_ref, hidden_ref, slope_ref, second_ref, gin_ref, gout_ref, all_ref
):
    rows = a_ref.shape[0] // 2
    gather_rows((a_ref.at[rows:], b_ref.at[rows:]), all_ref)

    def finish(i, here, gin, gout):
        gin_ref[here, :] = gin
        gout_ref[here, :] = gout

    weight_terms(second_ref, x_ref, all_ref, hidden_ref, slope_ref, finish)


def far_first_kernel(after_ref, x_over, diagonal_ref, first_ref, hidden_ref, slope_ref, x_ref):
    gather_rows((x_over, diagonal_ref.at[: x_over.shape[0]]), x_ref)
    gelu_rows(first_ref, x_ref, hidden_ref, slope_ref)


def far_second_kernel(
    after_ref,
    d_over,
    diagonal_ref,
    x_ref,
    hidden_ref,
    slope_ref,
    second_ref,
    gin_near,
    gout_near,
    gin_out,
    gout_out,
    d_ref,
    gin_ref,
    gout_ref,
    sems,
):
    gather_rows((d_over, diagonal_ref.at[d_over.shape[0] :]), d_ref)
    tile = second_ref.shape[0] // 2

    def copies(i):
        here = block(i, tile)
        return [
            pltpu.make_async_copy(gin_ref.at[here, :], gin_out.at[here, :], sems.at[i, 0]),
            pltpu.make_async_copy(gout_ref.at[here, :], gout_out.at[here, :], sems.at[i, 1]),
        ]

    def finish(i, here, gin, gout):
        gin_ref[here, :] = (gin_near[here, :] + gin).astype(gin_ref.dtype)
        gout_ref[here, :] = (gout_near[here, :] + gout).astype(gout_ref.dtype)
        for copy in copies(i):
            copy.start()

    weight_terms(second_ref, x_ref, d_ref, hidden_ref, slope_ref, finish)
    for i in range(2):
        for copy in copies(i):
            copy.wait()


def unpack_kernel(
    cap_rows, after_ref, back_ref, gate_ref, expert_ref, slot_ref, tok_ref, dgate_ref
):
    experts = back_ref.shape[0]
    blocks = tok_ref.shape[1] // LANES
    lane = lax.broadcasted_iota(jnp.int32, (SUBLANES, LANES), 1)
    rows, gates = [], []
    for e in range(experts):
        value = back_ref[e].astype(jnp.float32)
        pieces = [value[i * cap_rows : (i + 1) * cap_rows] for i in range(blocks)]
        rows.append(jnp.concatenate(pieces, axis=1))
        tail = value[cap_rows * blocks :]
        gates += [jnp.where(lane == i, tail, 0.0) for i in range(cap_rows // SUBLANES)]
    rows = jnp.concatenate(rows, axis=0).astype(jnp.bfloat16)
    gates = jnp.concatenate(gates, axis=0).astype(jnp.bfloat16)
    chosen = owner_table(expert_ref[...], slot_ref[...], cap_rows, experts * cap_rows)
    table = chosen.astype(jnp.bfloat16)
    tok_ref[...] = dot_tn(table, rows).astype(jnp.bfloat16)
    picked = jnp.sum(dot_tn(gates, table), axis=0, keepdims=True)
    dgate_ref[...] = picked / gate_ref[...]


def in_hbm(*arrays):
    return [pltpu.with_memory_space_constraint(a, pltpu.HBM) for a in arrays]


def body(tokens, upstream, gate_prob, expert_id, slot_index, segment_id, weight_in, weight_out):
    experts = lax.axis_size("expert")
    groups = lax.axis_size("dp")
    tok_rows, width = tokens.shape
    hidden_units = weight_in.shape[1]
    capacity = 5 * tok_rows // (4 * experts)
    cap_rows = -(-capacity // SUBLANES) * SUBLANES
    slots = experts * cap_rows
    share = hidden_units // groups
    gate_row = gate_prob.reshape(1, tok_rows)
    expert_row = expert_id.reshape(1, tok_rows)
    slot_row = slot_index.reshape(1, tok_rows)
    pairs = experts // 2
    which = lax.axis_index("dp").astype(jnp.int32).reshape(1)
    me = lax.axis_index("expert").astype(jnp.int32).reshape(1)
    bf16 = jnp.bfloat16
    anywhere = pl.BlockSpec(memory_space=pl.ANY)
    smem = pl.BlockSpec(memory_space=pltpu.SMEM)
    vmem = pl.BlockSpec(memory_space=pltpu.VMEM)

    unit = 2 * slots * width * hidden_units

    def call(kernel, name, ins, outs, scratch=(), out_spec=vmem, limit=10, work=0.0):
        return pl.pallas_call(
            kernel,
            in_specs=ins,
            out_specs=[out_spec] * len(outs),
            out_shape=[jax.ShapeDtypeStruct(shape, dtype) for shape, dtype in outs],
            scratch_shapes=list(scratch),
            compiler_params=pltpu.CompilerParams(vmem_limit_bytes=limit * MIB),
            cost_estimate=pl.CostEstimate(
                flops=int(work * unit), bytes_accessed=int(work * unit) // 512, transcendentals=0
            ),
            name=name,
        )

    def across(chunk, mask):
        return lax.ppermute(chunk, "expert", [(i, i ^ mask) for i in range(experts)])

    def over(chunk, mask):
        return lax.ppermute(chunk, "dp", [(i, i ^ mask) for i in range(groups)])

    row = (1, tok_rows)
    part = ((2 * cap_rows, width), bf16)
    half = ((pairs * cap_rows, width), bf16)
    *x_parts, d_keep, d_cross = call(
        partial(pack_kernel, cap_rows, experts),
        "pack",
        [smem] + [anywhere] * 6,
        [part] * pairs + [half] * 2,
        [
            pltpu.VMEM((tok_rows, width), bf16),
            pltpu.VMEM((tok_rows, width), bf16),
            pltpu.VMEM(row, jnp.float32),
            pltpu.VMEM(row, jnp.int32),
            pltpu.VMEM(row, jnp.int32),
            pltpu.VMEM(row, jnp.int32),
            pltpu.SemaphoreType.DMA((6,)),
        ],
    )(me, *in_hbm(tokens, upstream, gate_row, expert_row, slot_row, segment_id))
    order = list(range(pairs - 1, 0, -1))
    x_near = {s: across(x_parts[s], 2 * s) for s in order}
    x_near = [x_parts[0]] + [x_near[s] for s in range(1, pairs)]
    d_near = across(d_cross, 1)
    d_parts = call(
        partial(turn_d_kernel, pairs),
        "turn_d",
        [vmem] * 2,
        [part] * pairs,
    )(d_keep, d_near)
    x_keep, x_cross = call(
        turn_x_kernel,
        "turn_x",
        [anywhere] + [vmem] * pairs,
        [half] * 2,
    )(d_parts[0], *x_near)
    d_far = {s: across(d_parts[s], 2 * s) for s in order}
    d_far = [d_parts[0]] + [d_far[s] for s in range(1, pairs)]
    x_own = jnp.concatenate([x_keep, across(x_cross, 1)], axis=0)

    steps = groups
    wide = ((steps, slots, share), bf16)
    weights = pltpu.VMEM((hidden_units, width), bf16)
    hidden, slope = call(
        own_first_kernel,
        "own_first",
        [vmem, anywhere],
        [wide] * 2,
        [weights, pltpu.SemaphoreType.DMA((steps, 1))],
        limit=14,
        work=1,
    )(x_own, *in_hbm(weight_in[0]))
    pair_rows = ((2 * slots, width), bf16)
    (own,) = call(
        join_kernel,
        "join",
        [anywhere] + [vmem] * (pairs + 1),
        [pair_rows],
    )(hidden, x_own, *d_far)
    x_over, d_over, core = over(x_own, 2), over(own[slots:], 2), over(own, 1)

    stride = cap_rows * width // LANES + SUBLANES
    (back,) = call(
        partial(own_second_kernel, cap_rows),
        "own_second",
        [smem] + [vmem] * 4 + [anywhere],
        [((experts, stride, LANES), bf16)],
        [
            pltpu.VMEM((slots, width), jnp.float32),
            pltpu.VMEM((slots, LANES), jnp.float32),
            pltpu.VMEM((experts, stride, LANES), bf16),
            weights,
            pltpu.SemaphoreType.DMA((steps, 1)),
            pltpu.SemaphoreType.DMA((experts,)),
        ],
        out_spec=anywhere,
        limit=14,
        work=20,
    )(me, own, hidden, slope, weight_out[0], *in_hbm(weight_in[0]))
    returned = lax.all_to_all(back, "expert", split_axis=0, concat_axis=0, tiled=True)

    wide = ((share, 2 * slots), bf16)
    share_rows = ((share, width), bf16)
    term = ((share, width), jnp.float32)
    hidden_t, slope_t, x_near, first_share, second_share = call(
        near_first_kernel,
        "near_first",
        [smem] + [anywhere] + [vmem] * 2 + [anywhere] * 2,
        [wide, wide, pair_rows, share_rows, share_rows],
        [pltpu.SemaphoreType.DMA((2,))],
        work=0.5,
    )(which, back, own, core, *in_hbm(weight_in[0], weight_out[0]))
    gin_near, gout_near = call(
        near_second_kernel,
        "near_second",
        [anywhere] + [vmem] * 6,
        [term, term],
        [pltpu.VMEM(*pair_rows)],
        work=15,
    )(back, own, core, x_near, hidden_t, slope_t, second_share)
    (moved,) = call(
        forward_kernel,
        "forward",
        [anywhere, vmem, vmem],
        [pair_rows],
    )(hidden_t, x_over, d_over)
    diagonal = over(moved, 1)
    hidden_t, slope_t, x_far = call(
        far_first_kernel,
        "far_first",
        [anywhere] + [vmem] * 3,
        [wide, wide, pair_rows],
    )(gin_near, x_over, diagonal, first_share)
    share_block = pltpu.VMEM((share, width), bf16)
    grad_first, grad_second = call(
        far_second_kernel,
        "far_second",
        [anywhere] + [vmem] * 8,
        [share_rows] * 2,
        [pltpu.VMEM(*pair_rows), share_block, share_block, pltpu.SemaphoreType.DMA((2, 2))],
        out_spec=anywhere,
        limit=20,
    )(hidden_t, d_over, diagonal, x_far, hidden_t, slope_t, second_share, gin_near, gout_near)

    d_tokens, d_gate = call(
        partial(unpack_kernel, cap_rows),
        "unpack",
        [anywhere] + [vmem] * 4,
        [((tok_rows, width), bf16), (row, jnp.float32)],
    )(*in_hbm(grad_first), returned, gate_row, expert_row, slot_row)
    return (d_tokens, d_gate.reshape(tok_rows), grad_first[None], grad_second[None])


def solution(mesh):
    in_specs = (
        P(("dp", "expert"), None),
        P(("dp", "expert"), None),
        P(("dp", "expert")),
        P(("dp", "expert")),
        P(("dp", "expert")),
        P(("dp", "expert"), None),
        P("expert", None, None),
        P("expert", None, None),
    )
    out_specs = (
        P(("dp", "expert"), None),
        P(("dp", "expert")),
        P("expert", "dp", None),
        P("expert", "dp", None),
    )
    return jax.shard_map(body, mesh=mesh, in_specs=in_specs, out_specs=out_specs, check_vma=False)
```

```python
from functools import partial

import jax
import jax.numpy as jnp
from jax import lax
from jax.experimental import pallas as pl
from jax.experimental.pallas import tpu as pltpu
from jax.sharding import PartitionSpec as P

SEGS = 4
LANES = 128
SUBLANES = 8
MIB = 1024 * 1024
ROOT_2_PI = 0.7978845608028654
CUBIC = 0.044715


def dot_nn(a, b):
    return lax.dot_general(a, b, (((1,), (0,)), ((), ())), preferred_element_type=jnp.float32)


def dot_nt(a, b):
    return lax.dot_general(a, b, (((1,), (1,)), ((), ())), preferred_element_type=jnp.float32)


def dot_tn(a, b):
    return lax.dot_general(a, b, (((0,), (0,)), ((), ())), preferred_element_type=jnp.float32)


def gelu_and_slope(v):
    square = v * v
    t = jnp.tanh(v * (ROOT_2_PI + (ROOT_2_PI * CUBIC) * square))
    half = 0.5 + 0.5 * t
    hidden = v * half
    slope = half + hidden * (1.0 - t) * (ROOT_2_PI + (3.0 * ROOT_2_PI * CUBIC) * square)
    return hidden.astype(jnp.bfloat16), slope


def owner_table(chunk, slot, cap_rows, slots):
    place = jnp.where(slot >= 0, chunk * cap_rows + slot, -1)
    rows = lax.broadcasted_iota(jnp.int32, (slots, slot.shape[1]), 0)
    return rows == place


def pack_kernel(cap_rows, experts, me_ref, *refs):
    pairs = experts // 2
    sources, x_refs, (keep_ref, cross_ref) = refs[:6], refs[6 : 6 + pairs], refs[6 + pairs : 8 + pairs]
    scratch, sems = refs[8 + pairs : 14 + pairs], refs[14 + pairs]
    copies = [
        pltpu.make_async_copy(src, dst, sems.at[i])
        for i, (src, dst) in enumerate(zip(sources, scratch))
    ]
    for copy in copies:
        copy.start()
    for copy in copies:
        copy.wait()
    tok_ref, up_ref, gate_ref, expert_ref, slot_ref, seg_ref = scratch
    tok_rows = tok_ref.shape[0]
    slots = experts * cap_rows
    chunk, slot = expert_ref[...] ^ me_ref[0], slot_ref[...]
    table = owner_table(chunk, slot, cap_rows, slots).astype(jnp.bfloat16)
    split_rows(dot_nn(table, tok_ref[...]), x_refs)
    seg = seg_ref[...]
    length = jnp.zeros(seg.shape, jnp.float32)
    for label in range(SEGS):
        member = (seg == label).astype(jnp.float32)
        length = length + member * jnp.sum(member, axis=1, keepdims=True)
    weight = tok_rows / (SEGS * length)
    chosen = owner_table((chunk & 1) * pairs + (chunk >> 1), slot, cap_rows, slots)
    table = chosen.astype(jnp.bfloat16)
    weight_col = jnp.sum(jnp.where(chosen, weight, 0.0), axis=1, keepdims=True)
    gate_col = jnp.sum(jnp.where(chosen, gate_ref[...], 0.0), axis=1, keepdims=True)
    cotangent = (dot_nn(table, up_ref[...]) * weight_col).astype(jnp.bfloat16)
    split_rows(cotangent.astype(jnp.float32) * gate_col, (keep_ref, cross_ref))


def split_rows(value, refs):
    rows = value.shape[0] // len(refs)
    for i, ref in enumerate(refs):
        ref[...] = value[i * rows : (i + 1) * rows].astype(ref.dtype)


def halves(refs):
    values = [ref[...].astype(jnp.float32) for ref in refs]
    half = values[0].shape[0] // 2
    return [jnp.concatenate([v[b * half : (b + 1) * half] for v in values], axis=0) for b in (0, 1)]


def turn_d_kernel(pairs, keep_ref, near_ref, *out_refs):
    both = [ref[...].astype(jnp.float32) for ref in (keep_ref, near_ref)]
    rows = both[0].shape[0] // pairs
    for i, ref in enumerate(out_refs):
        ref[...] = jnp.concatenate([v[i * rows : (i + 1) * rows] for v in both], axis=0).astype(ref.dtype)


def turn_x_kernel(after_ref, *refs):
    for ref, value in zip(refs[-2:], halves(refs[:-2])):
        ref[...] = value.astype(ref.dtype)


def join_kernel(after_ref, x_ref, *refs):
    refs, own_ref = refs[:-1], refs[-1]
    rows = x_ref.shape[0]
    own_ref[:rows, :] = x_ref[...]
    own_ref[rows:, :] = jnp.concatenate(halves(refs), axis=0).astype(own_ref.dtype)


def copy_share(which_ref, source, target, sem):
    share = target.shape[0]
    start = pl.multiple_of(which_ref[0] * share, share)
    return pltpu.make_async_copy(source.at[pl.ds(start, share), :], target, sem)


def forward_kernel(after_ref, x_ref, d_ref, out_ref):
    gather_rows((x_ref, d_ref), out_ref)


def tile_copies(pairs, sems, i, tile):
    here = block(i, tile)
    return [
        pltpu.make_async_copy(source.at[here, :], target.at[here, :], sems.at[i, k])
        for k, (source, target) in enumerate(pairs)
    ]


def over_tiles(pairs, sems, steps, tile, work):
    for i in range(steps):
        for copy in tile_copies(pairs, sems, i, tile):
            copy.start()

    def step(i, carry):
        def arrived():
            for copy in tile_copies(pairs, sems, i, tile):
                copy.wait()

        work(i, arrived)
        return carry

    lax.fori_loop(0, steps, step, 0)


def own_first_kernel(rows_ref, first_src, hidden_ref, slope_ref, first_ref, sems):
    steps, tile = hidden_ref.shape[0], hidden_ref.shape[2]

    def work(i, arrived):
        arrived()
        hidden, slope = gelu_and_slope(dot_nt(rows_ref[...], first_ref[block(i, tile), :]))
        hidden_ref[i] = hidden
        slope_ref[i] = slope.astype(slope_ref.dtype)

    over_tiles([(first_src, first_ref)], sems, steps, tile, work)


def own_second_kernel(
    cap_rows,
    me_ref,
    own_ref,
    hidden_ref,
    slope_ref,
    second_ref,
    first_src,
    out_ref,
    total_ref,
    gate_ref,
    held_ref,
    first_ref,
    sems,
    out_sems,
):
    steps, tile = hidden_ref.shape[0], hidden_ref.shape[2]
    rows = total_ref.shape[0]

    def work(j, arrived):
        here = block(j, tile)
        back = dot_nt(own_ref[rows:, :], second_ref[here, :])
        terms = hidden_ref[j].astype(jnp.float32) * back
        gate = gate_ref[...]
        for i in range(tile // LANES):
            gate = gate + terms[:, i * LANES : (i + 1) * LANES]
        gate_ref[...] = gate
        d_pre = (back * slope_ref[j].astype(jnp.float32)).astype(jnp.bfloat16)
        arrived()
        total_ref[...] += dot_nn(d_pre, first_ref[here, :])

    total_ref[...] = jnp.zeros_like(total_ref)
    gate_ref[...] = jnp.zeros_like(gate_ref)
    over_tiles([(first_src, first_ref)], sems, steps, tile, work)

    experts, copies = out_ref.shape[0], []
    gates = jnp.sum(gate_ref[...], axis=1, keepdims=True)
    lane = lax.broadcasted_iota(jnp.int32, (SUBLANES, LANES), 1)
    for k in range(experts):
        start = k * cap_rows
        tail = jnp.zeros((SUBLANES, LANES), jnp.float32)
        for i in range(cap_rows // SUBLANES):
            here = start + i * SUBLANES
            tail = jnp.where(lane == i, gates[here : here + SUBLANES], tail)
        parts = [
            total_ref[start : start + cap_rows, i * LANES : (i + 1) * LANES]
            for i in range(total_ref.shape[1] // LANES)
        ]
        held_ref[k] = jnp.concatenate(parts + [tail], axis=0).astype(held_ref.dtype)
        source = me_ref[0] ^ (2 * (k % (experts // 2)) + k // (experts // 2))
        copies.append(pltpu.make_async_copy(held_ref.at[k], out_ref.at[source], out_sems.at[k]))
        copies[-1].start()
    for copy in copies:
        copy.wait()


def gather_rows(refs, all_ref):
    rows = refs[0].shape[0]
    for i, ref in enumerate(refs):
        all_ref[i * rows : (i + 1) * rows, :] = ref[...]


def block(i, tile=256):
    return pl.ds(pl.multiple_of(i * tile, tile), tile)


def gelu_rows(weights_ref, rows_ref, hidden_ref, slope_ref):
    tile = weights_ref.shape[0] // 2

    def step(i, carry):
        here = block(i, tile)
        hidden, slope = gelu_and_slope(dot_nt(weights_ref[here, :], rows_ref[...]))
        hidden_ref[here, :] = hidden
        slope_ref[here, :] = slope.astype(slope_ref.dtype)
        return carry

    lax.fori_loop(0, 2, step, 0)


def weight_terms(weights_ref, x_ref, d_ref, hidden_ref, slope_ref, finish):
    tile = weights_ref.shape[0] // 2

    def step(i, carry):
        here = block(i, tile)
        back = dot_nt(weights_ref[here, :], d_ref[...])
        d_pre = (back * slope_ref[here, :].astype(jnp.float32)).astype(jnp.bfloat16)
        finish(i, here, dot_nn(d_pre, x_ref[...]), dot_nn(hidden_ref[here, :], d_ref[...]))
        return carry

    lax.fori_loop(0, 2, step, 0)


def near_first_kernel(
    which_ref,
    after_ref,
    own,
    core,
    first_src,
    second_src,
    hidden_ref,
    slope_ref,
    x_ref,
    d_ref,
    first_ref,
    second_ref,
    sems,
):
    rows = x_ref.shape[0] // 2
    upper, lower = pl.ds(0, rows), pl.ds(rows, rows)
    now = [
        copy_share(which_ref, first_src, first_ref, sems.at[0]),
        pltpu.make_async_copy(own.at[upper, :], x_ref.at[upper, :], sems.at[1]),
        pltpu.make_async_copy(core.at[upper, :], x_ref.at[lower, :], sems.at[2]),
    ]
    later = [
        copy_share(which_ref, second_src, second_ref, sems.at[3]),
        pltpu.make_async_copy(own.at[lower, :], d_ref.at[upper, :], sems.at[4]),
        pltpu.make_async_copy(core.at[lower, :], d_ref.at[lower, :], sems.at[5]),
    ]
    for copy in now + later:
        copy.start()
    for copy in now:
        copy.wait()
    gelu_rows(first_ref, x_ref, hidden_ref, slope_ref)
    for copy in later:
        copy.wait()


def near_second_kernel(after_ref, x_ref, d_ref, hidden_ref, slope_ref, second_ref, gin_ref, gout_ref):
    def finish(i, here, gin, gout):
        gin_ref[here, :] = gin
        gout_ref[here, :] = gout

    weight_terms(second_ref, x_ref, d_ref, hidden_ref, slope_ref, finish)


def far_first_kernel(after_ref, x_over, diagonal_ref, first_ref, hidden_ref, slope_ref, x_ref):
    gather_rows((x_over, diagonal_ref.at[: x_over.shape[0]]), x_ref)
    gelu_rows(first_ref, x_ref, hidden_ref, slope_ref)


def far_second_kernel(
    after_ref,
    d_over,
    diagonal_ref,
    x_ref,
    hidden_ref,
    slope_ref,
    second_ref,
    gin_near,
    gout_near,
    gin_out,
    gout_out,
    d_ref,
    gin_ref,
    gout_ref,
    sems,
):
    gather_rows((d_over, diagonal_ref.at[d_over.shape[0] :]), d_ref)
    tile = second_ref.shape[0] // 2

    def copies(i):
        here = block(i, tile)
        return [
            pltpu.make_async_copy(gin_ref.at[here, :], gin_out.at[here, :], sems.at[i, 0]),
            pltpu.make_async_copy(gout_ref.at[here, :], gout_out.at[here, :], sems.at[i, 1]),
        ]

    def finish(i, here, gin, gout):
        gin_ref[here, :] = (gin_near[here, :] + gin).astype(gin_ref.dtype)
        gout_ref[here, :] = (gout_near[here, :] + gout).astype(gout_ref.dtype)
        for copy in copies(i):
            copy.start()

    weight_terms(second_ref, x_ref, d_ref, hidden_ref, slope_ref, finish)
    for i in range(2):
        for copy in copies(i):
            copy.wait()


def unpack_kernel(
    cap_rows, after_ref, back_ref, gate_ref, expert_ref, slot_ref, tok_ref, dgate_ref
):
    experts = back_ref.shape[0]
    blocks = tok_ref.shape[1] // LANES
    lane = lax.broadcasted_iota(jnp.int32, (SUBLANES, LANES), 1)
    rows, gates = [], []
    for e in range(experts):
        value = back_ref[e].astype(jnp.float32)
        pieces = [value[i * cap_rows : (i + 1) * cap_rows] for i in range(blocks)]
        rows.append(jnp.concatenate(pieces, axis=1))
        tail = value[cap_rows * blocks :]
        gates += [jnp.where(lane == i, tail, 0.0) for i in range(cap_rows // SUBLANES)]
    rows = jnp.concatenate(rows, axis=0).astype(jnp.bfloat16)
    gates = jnp.concatenate(gates, axis=0).astype(jnp.bfloat16)
    chosen = owner_table(expert_ref[...], slot_ref[...], cap_rows, experts * cap_rows)
    table = chosen.astype(jnp.bfloat16)
    tok_ref[...] = dot_tn(table, rows).astype(jnp.bfloat16)
    picked = jnp.sum(dot_tn(gates, table), axis=0, keepdims=True)
    dgate_ref[...] = picked / gate_ref[...]


def in_hbm(*arrays):
    return [pltpu.with_memory_space_constraint(a, pltpu.HBM) for a in arrays]


def body(tokens, upstream, gate_prob, expert_id, slot_index, segment_id, weight_in, weight_out):
    experts = lax.axis_size("expert")
    groups = lax.axis_size("dp")
    tok_rows, width = tokens.shape
    hidden_units = weight_in.shape[1]
    capacity = 5 * tok_rows // (4 * experts)
    cap_rows = -(-capacity // SUBLANES) * SUBLANES
    slots = experts * cap_rows
    share = hidden_units // groups
    gate_row = gate_prob.reshape(1, tok_rows)
    expert_row = expert_id.reshape(1, tok_rows)
    slot_row = slot_index.reshape(1, tok_rows)
    pairs = experts // 2
    which = lax.axis_index("dp").astype(jnp.int32).reshape(1)
    me = lax.axis_index("expert").astype(jnp.int32).reshape(1)
    bf16 = jnp.bfloat16
    anywhere = pl.BlockSpec(memory_space=pl.ANY)
    smem = pl.BlockSpec(memory_space=pltpu.SMEM)
    vmem = pl.BlockSpec(memory_space=pltpu.VMEM)

    unit = 2 * slots * width * hidden_units

    def call(kernel, name, ins, outs, scratch=(), out_spec=vmem, limit=10, work=0.0):
        return pl.pallas_call(
            kernel,
            in_specs=ins,
            out_specs=[out_spec] * len(outs),
            out_shape=[jax.ShapeDtypeStruct(shape, dtype) for shape, dtype in outs],
            scratch_shapes=list(scratch),
            compiler_params=pltpu.CompilerParams(vmem_limit_bytes=limit * MIB),
            cost_estimate=pl.CostEstimate(
                flops=int(work * unit), bytes_accessed=int(work * unit) // 512, transcendentals=0
            ),
            name=name,
        )

    def across(chunk, mask):
        return lax.ppermute(chunk, "expert", [(i, i ^ mask) for i in range(experts)])

    def over(chunk, mask):
        return lax.ppermute(chunk, "dp", [(i, i ^ mask) for i in range(groups)])

    row = (1, tok_rows)
    part = ((2 * cap_rows, width), bf16)
    half = ((pairs * cap_rows, width), bf16)
    *x_parts, d_keep, d_cross = call(
        partial(pack_kernel, cap_rows, experts),
        "pack",
        [smem] + [anywhere] * 6,
        [part] * pairs + [half] * 2,
        [
            pltpu.VMEM((tok_rows, width), bf16),
            pltpu.VMEM((tok_rows, width), bf16),
            pltpu.VMEM(row, jnp.float32),
            pltpu.VMEM(row, jnp.int32),
            pltpu.VMEM(row, jnp.int32),
            pltpu.VMEM(row, jnp.int32),
            pltpu.SemaphoreType.DMA((6,)),
        ],
    )(me, *in_hbm(tokens, upstream, gate_row, expert_row, slot_row, segment_id))
    order = list(range(pairs - 1, 0, -1))
    x_near = {s: across(x_parts[s], 2 * s) for s in order}
    x_near = [x_parts[0]] + [x_near[s] for s in range(1, pairs)]
    d_near = across(d_cross, 1)
    d_parts = call(
        partial(turn_d_kernel, pairs),
        "turn_d",
        [vmem] * 2,
        [part] * pairs,
    )(d_keep, d_near)
    x_keep, x_cross = call(
        turn_x_kernel,
        "turn_x",
        [anywhere] + [vmem] * pairs,
        [half] * 2,
    )(d_parts[0], *x_near)
    d_far = {s: across(d_parts[s], 2 * s) for s in order}
    d_far = [d_parts[0]] + [d_far[s] for s in range(1, pairs)]
    x_own = jnp.concatenate([x_keep, across(x_cross, 1)], axis=0)

    steps = groups
    wide = ((steps, slots, share), bf16)
    weights = pltpu.VMEM((hidden_units, width), bf16)
    hidden, slope = call(
        own_first_kernel,
        "own_first",
        [vmem, anywhere],
        [wide] * 2,
        [weights, pltpu.SemaphoreType.DMA((steps, 1))],
        limit=14,
        work=1,
    )(x_own, *in_hbm(weight_in[0]))
    pair_rows = ((2 * slots, width), bf16)
    (own,) = call(
        join_kernel,
        "join",
        [anywhere] + [vmem] * (pairs + 1),
        [pair_rows],
    )(hidden, x_own, *d_far)
    x_over, d_over, core = over(x_own, 2), over(own[slots:], 2), over(own, 1)

    stride = cap_rows * width // LANES + SUBLANES
    (back,) = call(
        partial(own_second_kernel, cap_rows),
        "own_second",
        [smem] + [vmem] * 4 + [anywhere],
        [((experts, stride, LANES), bf16)],
        [
            pltpu.VMEM((slots, width), jnp.float32),
            pltpu.VMEM((slots, LANES), jnp.float32),
            pltpu.VMEM((experts, stride, LANES), bf16),
            weights,
            pltpu.SemaphoreType.DMA((steps, 1)),
            pltpu.SemaphoreType.DMA((experts,)),
        ],
        out_spec=anywhere,
        limit=14,
        work=20,
    )(me, own, hidden, slope, weight_out[0], *in_hbm(weight_in[0]))
    returned = lax.all_to_all(back, "expert", split_axis=0, concat_axis=0, tiled=True)

    wide = ((share, 2 * slots), bf16)
    share_rows = ((share, width), bf16)
    term = ((share, width), jnp.float32)
    hidden_t, slope_t, x_near, d_near, first_share, second_share = call(
        near_first_kernel,
        "near_first",
        [smem] + [anywhere] * 5,
        [wide, wide, pair_rows, pair_rows, share_rows, share_rows],
        [pltpu.SemaphoreType.DMA((6,))],
        work=0.5,
    )(which, back, own, core, *in_hbm(weight_in[0], weight_out[0]))
    gin_near, gout_near = call(
        near_second_kernel,
        "near_second",
        [anywhere] + [vmem] * 5,
        [term, term],
        work=15,
    )(back, x_near, d_near, hidden_t, slope_t, second_share)
    (moved,) = call(
        forward_kernel,
        "forward",
        [anywhere, vmem, vmem],
        [pair_rows],
    )(hidden_t, x_over, d_over)
    diagonal = over(moved, 1)
    hidden_t, slope_t, x_far = call(
        far_first_kernel,
        "far_first",
        [anywhere] + [vmem] * 3,
        [wide, wide, pair_rows],
    )(gin_near, x_over, diagonal, first_share)
    share_block = pltpu.VMEM((share, width), bf16)
    grad_first, grad_second = call(
        far_second_kernel,
        "far_second",
        [anywhere] + [vmem] * 8,
        [share_rows] * 2,
        [pltpu.VMEM(*pair_rows), share_block, share_block, pltpu.SemaphoreType.DMA((2, 2))],
        out_spec=anywhere,
        limit=20,
    )(hidden_t, d_over, diagonal, x_far, hidden_t, slope_t, second_share, gin_near, gout_near)

    d_tokens, d_gate = call(
        partial(unpack_kernel, cap_rows),
        "unpack",
        [anywhere] + [vmem] * 4,
        [((tok_rows, width), bf16), (row, jnp.float32)],
    )(*in_hbm(grad_first), returned, gate_row, expert_row, slot_row)
    return (d_tokens, d_gate.reshape(tok_rows), grad_first[None], grad_second[None])


def solution(mesh):
    in_specs = (
        P(("dp", "expert"), None),
        P(("dp", "expert"), None),
        P(("dp", "expert")),
        P(("dp", "expert")),
        P(("dp", "expert")),
        P(("dp", "expert"), None),
        P("expert", None, None),
        P("expert", None, None),
    )
    out_specs = (
        P(("dp", "expert"), None),
        P(("dp", "expert")),
        P("expert", "dp", None),
        P("expert", "dp", None),
    )
    return jax.shard_map(body, mesh=mesh, in_specs=in_specs, out_specs=out_specs, check_vma=False)
```

```python
from functools import partial

import jax
import jax.numpy as jnp
from jax import lax
from jax.experimental import pallas as pl
from jax.experimental.pallas import tpu as pltpu
from jax.sharding import PartitionSpec as P

SEGS = 4
LANES = 128
SUBLANES = 8
MIB = 1024 * 1024
ROOT_2_PI = 0.7978845608028654
CUBIC = 0.044715


def dot_nn(a, b):
    return lax.dot_general(a, b, (((1,), (0,)), ((), ())), preferred_element_type=jnp.float32)


def dot_nt(a, b):
    return lax.dot_general(a, b, (((1,), (1,)), ((), ())), preferred_element_type=jnp.float32)


def dot_tn(a, b):
    return lax.dot_general(a, b, (((0,), (0,)), ((), ())), preferred_element_type=jnp.float32)


def gelu_and_slope(v):
    square = v * v
    t = jnp.tanh(v * (ROOT_2_PI + (ROOT_2_PI * CUBIC) * square))
    half = 0.5 + 0.5 * t
    hidden = v * half
    slope = half + hidden * (1.0 - t) * (ROOT_2_PI + (3.0 * ROOT_2_PI * CUBIC) * square)
    return hidden.astype(jnp.bfloat16), slope


def owner_table(chunk, slot, cap_rows, slots):
    place = jnp.where(slot >= 0, chunk * cap_rows + slot, -1)
    rows = lax.broadcasted_iota(jnp.int32, (slots, slot.shape[1]), 0)
    return rows == place


def pack_kernel(cap_rows, experts, me_ref, *refs):
    pairs = experts // 2
    sources, x_refs, (keep_ref, cross_ref) = refs[:6], refs[6 : 6 + pairs], refs[6 + pairs : 8 + pairs]
    scratch, sems = refs[8 + pairs : 14 + pairs], refs[14 + pairs]
    copies = [
        pltpu.make_async_copy(src, dst, sems.at[i])
        for i, (src, dst) in enumerate(zip(sources, scratch))
    ]
    for copy in copies:
        copy.start()
    for copy in copies:
        copy.wait()
    tok_ref, up_ref, gate_ref, expert_ref, slot_ref, seg_ref = scratch
    tok_rows = tok_ref.shape[0]
    slots = experts * cap_rows
    chunk, slot = expert_ref[...] ^ me_ref[0], slot_ref[...]
    table = owner_table(chunk, slot, cap_rows, slots).astype(jnp.bfloat16)
    split_rows(dot_nn(table, tok_ref[...]), x_refs)
    seg = seg_ref[...]
    length = jnp.zeros(seg.shape, jnp.float32)
    for label in range(SEGS):
        member = (seg == label).astype(jnp.float32)
        length = length + member * jnp.sum(member, axis=1, keepdims=True)
    weight = tok_rows / (SEGS * length)
    chosen = owner_table((chunk & 1) * pairs + (chunk >> 1), slot, cap_rows, slots)
    table = chosen.astype(jnp.bfloat16)
    weight_col = jnp.sum(jnp.where(chosen, weight, 0.0), axis=1, keepdims=True)
    gate_col = jnp.sum(jnp.where(chosen, gate_ref[...], 0.0), axis=1, keepdims=True)
    cotangent = (dot_nn(table, up_ref[...]) * weight_col).astype(jnp.bfloat16)
    split_rows(cotangent.astype(jnp.float32) * gate_col, (keep_ref, cross_ref))


def split_rows(value, refs):
    rows = value.shape[0] // len(refs)
    for i, ref in enumerate(refs):
        ref[...] = value[i * rows : (i + 1) * rows].astype(ref.dtype)


def halves(refs):
    values = [ref[...].astype(jnp.float32) for ref in refs]
    half = values[0].shape[0] // 2
    return [jnp.concatenate([v[b * half : (b + 1) * half] for v in values], axis=0) for b in (0, 1)]


def turn_d_kernel(pairs, keep_ref, near_ref, *out_refs):
    both = [ref[...].astype(jnp.float32) for ref in (keep_ref, near_ref)]
    rows = both[0].shape[0] // pairs
    for i, ref in enumerate(out_refs):
        ref[...] = jnp.concatenate([v[i * rows : (i + 1) * rows] for v in both], axis=0).astype(ref.dtype)


def turn_x_kernel(after_ref, *refs):
    for ref, value in zip(refs[-2:], halves(refs[:-2])):
        ref[...] = value.astype(ref.dtype)


def join_kernel(after_ref, x_ref, *refs):
    refs, own_ref = refs[:-1], refs[-1]
    rows = x_ref.shape[0]
    own_ref[:rows, :] = x_ref[...]
    own_ref[rows:, :] = jnp.concatenate(halves(refs), axis=0).astype(own_ref.dtype)


def copy_share(which_ref, source, target, sem):
    share = target.shape[0]
    start = pl.multiple_of(which_ref[0] * share, share)
    return pltpu.make_async_copy(source.at[pl.ds(start, share), :], target, sem)


def forward_kernel(after_ref, x_ref, d_ref, out_ref):
    gather_rows((x_ref, d_ref), out_ref)


def own_first_kernel(rows_ref, first_ref, hidden_ref, slope_ref):
    steps, tile = hidden_ref.shape[0], hidden_ref.shape[2]

    def step(i, carry):
        hidden, slope = gelu_and_slope(dot_nt(rows_ref[...], first_ref[block(i, tile), :]))
        hidden_ref[i] = hidden
        slope_ref[i] = slope.astype(slope_ref.dtype)
        return carry

    lax.fori_loop(0, steps, step, 0)


def own_second_kernel(
    cap_rows,
    me_ref,
    own_ref,
    hidden_ref,
    slope_ref,
    second_ref,
    first_ref,
    out_ref,
    total_ref,
    gate_ref,
    held_ref,
    out_sems,
):
    steps, tile = hidden_ref.shape[0], hidden_ref.shape[2]
    rows = total_ref.shape[0]

    def step(j, carry):
        here = block(j, tile)
        back = dot_nt(own_ref[rows:, :], second_ref[here, :])
        terms = hidden_ref[j].astype(jnp.float32) * back
        gate = gate_ref[...]
        for i in range(tile // LANES):
            gate = gate + terms[:, i * LANES : (i + 1) * LANES]
        gate_ref[...] = gate
        d_pre = (back * slope_ref[j].astype(jnp.float32)).astype(jnp.bfloat16)
        total_ref[...] += dot_nn(d_pre, first_ref[here, :])
        return carry

    total_ref[...] = jnp.zeros_like(total_ref)
    gate_ref[...] = jnp.zeros_like(gate_ref)
    lax.fori_loop(0, steps, step, 0)

    experts, copies = out_ref.shape[0], []
    gates = jnp.sum(gate_ref[...], axis=1, keepdims=True)
    lane = lax.broadcasted_iota(jnp.int32, (SUBLANES, LANES), 1)
    for k in range(experts):
        start = k * cap_rows
        tail = jnp.zeros((SUBLANES, LANES), jnp.float32)
        for i in range(cap_rows // SUBLANES):
            here = start + i * SUBLANES
            tail = jnp.where(lane == i, gates[here : here + SUBLANES], tail)
        parts = [
            total_ref[start : start + cap_rows, i * LANES : (i + 1) * LANES]
            for i in range(total_ref.shape[1] // LANES)
        ]
        held_ref[k] = jnp.concatenate(parts + [tail], axis=0).astype(held_ref.dtype)
        source = me_ref[0] ^ (2 * (k % (experts // 2)) + k // (experts // 2))
        copies.append(pltpu.make_async_copy(held_ref.at[k], out_ref.at[source], out_sems.at[k]))
        copies[-1].start()
    for copy in copies:
        copy.wait()


def gather_rows(refs, all_ref):
    rows = refs[0].shape[0]
    for i, ref in enumerate(refs):
        all_ref[i * rows : (i + 1) * rows, :] = ref[...]


def block(i, tile=256):
    return pl.ds(pl.multiple_of(i * tile, tile), tile)


def gelu_rows(weights_ref, rows_ref, hidden_ref, slope_ref):
    tile = weights_ref.shape[0] // 2

    def step(i, carry):
        here = block(i, tile)
        hidden, slope = gelu_and_slope(dot_nt(weights_ref[here, :], rows_ref[...]))
        hidden_ref[here, :] = hidden
        slope_ref[here, :] = slope.astype(slope_ref.dtype)
        return carry

    lax.fori_loop(0, 2, step, 0)


def weight_terms(weights_ref, x_ref, d_ref, hidden_ref, slope_ref, finish):
    tile = weights_ref.shape[0] // 2

    def step(i, carry):
        here = block(i, tile)
        back = dot_nt(weights_ref[here, :], d_ref[...])
        d_pre = (back * slope_ref[here, :].astype(jnp.float32)).astype(jnp.bfloat16)
        finish(i, here, dot_nn(d_pre, x_ref[...]), dot_nn(hidden_ref[here, :], d_ref[...]))
        return carry

    lax.fori_loop(0, 2, step, 0)


def near_first_kernel(
    which_ref,
    after_ref,
    own,
    core,
    first_src,
    second_src,
    hidden_ref,
    slope_ref,
    x_ref,
    d_ref,
    first_ref,
    second_ref,
    sems,
):
    rows = x_ref.shape[0] // 2
    upper, lower = pl.ds(0, rows), pl.ds(rows, rows)
    now = [
        copy_share(which_ref, first_src, first_ref, sems.at[0]),
        pltpu.make_async_copy(own.at[upper, :], x_ref.at[upper, :], sems.at[1]),
        pltpu.make_async_copy(core.at[upper, :], x_ref.at[lower, :], sems.at[2]),
    ]
    later = [
        copy_share(which_ref, second_src, second_ref, sems.at[3]),
        pltpu.make_async_copy(own.at[lower, :], d_ref.at[upper, :], sems.at[4]),
        pltpu.make_async_copy(core.at[lower, :], d_ref.at[lower, :], sems.at[5]),
    ]
    for copy in now + later:
        copy.start()
    for copy in now:
        copy.wait()
    gelu_rows(first_ref, x_ref, hidden_ref, slope_ref)
    for copy in later:
        copy.wait()


def near_second_kernel(after_ref, x_ref, d_ref, hidden_ref, slope_ref, second_ref, gin_ref, gout_ref):
    def finish(i, here, gin, gout):
        gin_ref[here, :] = gin
        gout_ref[here, :] = gout

    weight_terms(second_ref, x_ref, d_ref, hidden_ref, slope_ref, finish)


def far_first_kernel(after_ref, x_over, diagonal_ref, first_ref, hidden_ref, slope_ref, x_ref):
    gather_rows((x_over, diagonal_ref.at[: x_over.shape[0]]), x_ref)
    gelu_rows(first_ref, x_ref, hidden_ref, slope_ref)


def far_second_kernel(
    after_ref,
    d_over,
    diagonal_ref,
    x_ref,
    hidden_ref,
    slope_ref,
    second_ref,
    gin_near,
    gout_near,
    gin_out,
    gout_out,
    d_ref,
    gin_ref,
    gout_ref,
    sems,
):
    gather_rows((d_over, diagonal_ref.at[d_over.shape[0] :]), d_ref)
    tile = second_ref.shape[0] // 2

    def copies(i):
        here = block(i, tile)
        return [
            pltpu.make_async_copy(gin_ref.at[here, :], gin_out.at[here, :], sems.at[i, 0]),
            pltpu.make_async_copy(gout_ref.at[here, :], gout_out.at[here, :], sems.at[i, 1]),
        ]

    def finish(i, here, gin, gout):
        gin_ref[here, :] = (gin_near[here, :] + gin).astype(gin_ref.dtype)
        gout_ref[here, :] = (gout_near[here, :] + gout).astype(gout_ref.dtype)
        for copy in copies(i):
            copy.start()

    weight_terms(second_ref, x_ref, d_ref, hidden_ref, slope_ref, finish)
    for i in range(2):
        for copy in copies(i):
            copy.wait()


def unpack_kernel(
    cap_rows, after_ref, back_ref, gate_ref, expert_ref, slot_ref, tok_ref, dgate_ref
):
    experts = back_ref.shape[0]
    blocks = tok_ref.shape[1] // LANES
    lane = lax.broadcasted_iota(jnp.int32, (SUBLANES, LANES), 1)
    rows, gates = [], []
    for e in range(experts):
        value = back_ref[e].astype(jnp.float32)
        pieces = [value[i * cap_rows : (i + 1) * cap_rows] for i in range(blocks)]
        rows.append(jnp.concatenate(pieces, axis=1))
        tail = value[cap_rows * blocks :]
        gates += [jnp.where(lane == i, tail, 0.0) for i in range(cap_rows // SUBLANES)]
    rows = jnp.concatenate(rows, axis=0).astype(jnp.bfloat16)
    gates = jnp.concatenate(gates, axis=0).astype(jnp.bfloat16)
    chosen = owner_table(expert_ref[...], slot_ref[...], cap_rows, experts * cap_rows)
    table = chosen.astype(jnp.bfloat16)
    tok_ref[...] = dot_tn(table, rows).astype(jnp.bfloat16)
    picked = jnp.sum(dot_tn(gates, table), axis=0, keepdims=True)
    dgate_ref[...] = picked / gate_ref[...]


def in_hbm(*arrays):
    return [pltpu.with_memory_space_constraint(a, pltpu.HBM) for a in arrays]


def body(tokens, upstream, gate_prob, expert_id, slot_index, segment_id, weight_in, weight_out):
    experts = lax.axis_size("expert")
    groups = lax.axis_size("dp")
    tok_rows, width = tokens.shape
    hidden_units = weight_in.shape[1]
    capacity = 5 * tok_rows // (4 * experts)
    cap_rows = -(-capacity // SUBLANES) * SUBLANES
    slots = experts * cap_rows
    share = hidden_units // groups
    gate_row = gate_prob.reshape(1, tok_rows)
    expert_row = expert_id.reshape(1, tok_rows)
    slot_row = slot_index.reshape(1, tok_rows)
    pairs = experts // 2
    which = lax.axis_index("dp").astype(jnp.int32).reshape(1)
    me = lax.axis_index("expert").astype(jnp.int32).reshape(1)
    bf16 = jnp.bfloat16
    anywhere = pl.BlockSpec(memory_space=pl.ANY)
    smem = pl.BlockSpec(memory_space=pltpu.SMEM)
    vmem = pl.BlockSpec(memory_space=pltpu.VMEM)

    unit = 2 * slots * width * hidden_units

    def call(kernel, name, ins, outs, scratch=(), out_spec=vmem, limit=10, work=0.0):
        return pl.pallas_call(
            kernel,
            in_specs=ins,
            out_specs=[out_spec] * len(outs),
            out_shape=[jax.ShapeDtypeStruct(shape, dtype) for shape, dtype in outs],
            scratch_shapes=list(scratch),
            compiler_params=pltpu.CompilerParams(vmem_limit_bytes=limit * MIB),
            cost_estimate=pl.CostEstimate(
                flops=int(work * unit), bytes_accessed=int(work * unit) // 512, transcendentals=0
            ),
            name=name,
        )

    def across(chunk, mask):
        return lax.ppermute(chunk, "expert", [(i, i ^ mask) for i in range(experts)])

    def over(chunk, mask):
        return lax.ppermute(chunk, "dp", [(i, i ^ mask) for i in range(groups)])

    row = (1, tok_rows)
    part = ((2 * cap_rows, width), bf16)
    half = ((pairs * cap_rows, width), bf16)
    *x_parts, d_keep, d_cross = call(
        partial(pack_kernel, cap_rows, experts),
        "pack",
        [smem] + [anywhere] * 6,
        [part] * pairs + [half] * 2,
        [
            pltpu.VMEM((tok_rows, width), bf16),
            pltpu.VMEM((tok_rows, width), bf16),
            pltpu.VMEM(row, jnp.float32),
            pltpu.VMEM(row, jnp.int32),
            pltpu.VMEM(row, jnp.int32),
            pltpu.VMEM(row, jnp.int32),
            pltpu.SemaphoreType.DMA((6,)),
        ],
    )(me, *in_hbm(tokens, upstream, gate_row, expert_row, slot_row, segment_id))
    order = list(range(pairs - 1, 0, -1))
    x_near = {s: across(x_parts[s], 2 * s) for s in order}
    x_near = [x_parts[0]] + [x_near[s] for s in range(1, pairs)]
    d_near = across(d_cross, 1)
    d_parts = call(
        partial(turn_d_kernel, pairs),
        "turn_d",
        [vmem] * 2,
        [part] * pairs,
    )(d_keep, d_near)
    x_keep, x_cross = call(
        turn_x_kernel,
        "turn_x",
        [anywhere] + [vmem] * pairs,
        [half] * 2,
    )(d_parts[0], *x_near)
    d_far = {s: across(d_parts[s], 2 * s) for s in order}
    d_far = [d_parts[0]] + [d_far[s] for s in range(1, pairs)]
    x_own = jnp.concatenate([x_keep, across(x_cross, 1)], axis=0)

    steps = hidden_units // 1024
    wide = ((steps, slots, 1024), bf16)
    hidden, slope = call(
        own_first_kernel,
        "own_first",
        [vmem] * 2,
        [wide] * 2,
        limit=12,
        work=1,
    )(x_own, weight_in[0])
    pair_rows = ((2 * slots, width), bf16)
    (own,) = call(
        join_kernel,
        "join",
        [anywhere] + [vmem] * (pairs + 1),
        [pair_rows],
    )(hidden, x_own, *d_far)
    x_over, d_over, core = over(x_own, 2), over(own[slots:], 2), over(own, 1)

    stride = cap_rows * width // LANES + SUBLANES
    (back,) = call(
        partial(own_second_kernel, cap_rows),
        "own_second",
        [smem] + [vmem] * 5,
        [((experts, stride, LANES), bf16)],
        [
            pltpu.VMEM((slots, width), jnp.float32),
            pltpu.VMEM((slots, LANES), jnp.float32),
            pltpu.VMEM((experts, stride, LANES), bf16),
            pltpu.SemaphoreType.DMA((experts,)),
        ],
        out_spec=anywhere,
        limit=16,
        work=20,
    )(me, own, hidden, slope, weight_out[0], weight_in[0])
    returned = lax.all_to_all(back, "expert", split_axis=0, concat_axis=0, tiled=True)

    wide = ((share, 2 * slots), bf16)
    share_rows = ((share, width), bf16)
    term = ((share, width), jnp.float32)
    hidden_t, slope_t, x_near, d_near, first_share, second_share = call(
        near_first_kernel,
        "near_first",
        [smem] + [anywhere] * 5,
        [wide, wide, pair_rows, pair_rows, share_rows, share_rows],
        [pltpu.SemaphoreType.DMA((6,))],
        work=0.5,
    )(which, back, own, core, *in_hbm(weight_in[0], weight_out[0]))
    gin_near, gout_near = call(
        near_second_kernel,
        "near_second",
        [anywhere] + [vmem] * 5,
        [term, term],
        work=15,
    )(back, x_near, d_near, hidden_t, slope_t, second_share)
    (moved,) = call(
        forward_kernel,
        "forward",
        [anywhere, vmem, vmem],
        [pair_rows],
    )(hidden_t, x_over, d_over)
    diagonal = over(moved, 1)
    hidden_t, slope_t, x_far = call(
        far_first_kernel,
        "far_first",
        [anywhere] + [vmem] * 3,
        [wide, wide, pair_rows],
    )(gin_near, x_over, diagonal, first_share)
    share_block = pltpu.VMEM((share, width), bf16)
    grad_first, grad_second = call(
        far_second_kernel,
        "far_second",
        [anywhere] + [vmem] * 8,
        [share_rows] * 2,
        [pltpu.VMEM(*pair_rows), share_block, share_block, pltpu.SemaphoreType.DMA((2, 2))],
        out_spec=anywhere,
        limit=20,
    )(hidden_t, d_over, diagonal, x_far, hidden_t, slope_t, second_share, gin_near, gout_near)

    d_tokens, d_gate = call(
        partial(unpack_kernel, cap_rows),
        "unpack",
        [anywhere] + [vmem] * 4,
        [((tok_rows, width), bf16), (row, jnp.float32)],
    )(*in_hbm(grad_first), returned, gate_row, expert_row, slot_row)
    return (d_tokens, d_gate.reshape(tok_rows), grad_first[None], grad_second[None])


def solution(mesh):
    in_specs = (
        P(("dp", "expert"), None),
        P(("dp", "expert"), None),
        P(("dp", "expert")),
        P(("dp", "expert")),
        P(("dp", "expert")),
        P(("dp", "expert"), None),
        P("expert", None, None),
        P("expert", None, None),
    )
    out_specs = (
        P(("dp", "expert"), None),
        P(("dp", "expert")),
        P("expert", "dp", None),
        P("expert", "dp", None),
    )
    return jax.shard_map(body, mesh=mesh, in_specs=in_specs, out_specs=out_specs, check_vma=False)
```

```python
from functools import partial

import jax
import jax.numpy as jnp
from jax import lax
from jax.experimental import pallas as pl
from jax.experimental.pallas import tpu as pltpu
from jax.sharding import PartitionSpec as P

SEGS = 4
LANES = 128
SUBLANES = 8
MIB = 1024 * 1024
ROOT_2_PI = 0.7978845608028654
CUBIC = 0.044715


def dot_nn(a, b):
    return lax.dot_general(a, b, (((1,), (0,)), ((), ())), preferred_element_type=jnp.float32)


def dot_nt(a, b):
    return lax.dot_general(a, b, (((1,), (1,)), ((), ())), preferred_element_type=jnp.float32)


def dot_tn(a, b):
    return lax.dot_general(a, b, (((0,), (0,)), ((), ())), preferred_element_type=jnp.float32)


def gelu_and_slope(v):
    square = v * v
    t = jnp.tanh(v * (ROOT_2_PI + (ROOT_2_PI * CUBIC) * square))
    half = 0.5 + 0.5 * t
    hidden = v * half
    slope = half + hidden * (1.0 - t) * (ROOT_2_PI + (3.0 * ROOT_2_PI * CUBIC) * square)
    return hidden.astype(jnp.bfloat16), slope


def owner_table(chunk, slot, cap_rows, slots):
    place = jnp.where(slot >= 0, chunk * cap_rows + slot, -1)
    rows = lax.broadcasted_iota(jnp.int32, (slots, slot.shape[1]), 0)
    return rows == place


def pack_kernel(cap_rows, experts, me_ref, *refs):
    pairs = experts // 2
    sources, x_refs, (keep_ref, cross_ref) = refs[:6], refs[6 : 6 + pairs], refs[6 + pairs : 8 + pairs]
    scratch, sems = refs[8 + pairs : 14 + pairs], refs[14 + pairs]
    copies = [
        pltpu.make_async_copy(src, dst, sems.at[i])
        for i, (src, dst) in enumerate(zip(sources, scratch))
    ]
    for copy in copies:
        copy.start()
    for copy in copies:
        copy.wait()
    tok_ref, up_ref, gate_ref, expert_ref, slot_ref, seg_ref = scratch
    tok_rows = tok_ref.shape[0]
    slots = experts * cap_rows
    chunk, slot = expert_ref[...] ^ me_ref[0], slot_ref[...]
    table = owner_table(chunk, slot, cap_rows, slots).astype(jnp.bfloat16)
    split_rows(dot_nn(table, tok_ref[...]), x_refs)
    seg = seg_ref[...]
    length = jnp.zeros(seg.shape, jnp.float32)
    for label in range(SEGS):
        member = (seg == label).astype(jnp.float32)
        length = length + member * jnp.sum(member, axis=1, keepdims=True)
    weight = tok_rows / (SEGS * length)
    chosen = owner_table((chunk & 1) * pairs + (chunk >> 1), slot, cap_rows, slots)
    table = chosen.astype(jnp.bfloat16)
    weight_col = jnp.sum(jnp.where(chosen, weight, 0.0), axis=1, keepdims=True)
    gate_col = jnp.sum(jnp.where(chosen, gate_ref[...], 0.0), axis=1, keepdims=True)
    cotangent = (dot_nn(table, up_ref[...]) * weight_col).astype(jnp.bfloat16)
    split_rows(cotangent.astype(jnp.float32) * gate_col, (keep_ref, cross_ref))


def split_rows(value, refs):
    rows = value.shape[0] // len(refs)
    for i, ref in enumerate(refs):
        ref[...] = value[i * rows : (i + 1) * rows].astype(ref.dtype)


def halves(refs):
    values = [ref[...].astype(jnp.float32) for ref in refs]
    half = values[0].shape[0] // 2
    return [jnp.concatenate([v[b * half : (b + 1) * half] for v in values], axis=0) for b in (0, 1)]


def turn_d_kernel(pairs, keep_ref, near_ref, *out_refs):
    both = [ref[...].astype(jnp.float32) for ref in (keep_ref, near_ref)]
    rows = both[0].shape[0] // pairs
    for i, ref in enumerate(out_refs):
        ref[...] = jnp.concatenate([v[i * rows : (i + 1) * rows] for v in both], axis=0).astype(ref.dtype)


def turn_x_kernel(after_ref, *refs):
    for ref, value in zip(refs[-2:], halves(refs[:-2])):
        ref[...] = value.astype(ref.dtype)


def join_kernel(after_ref, x_ref, *refs):
    refs, own_ref = refs[:-1], refs[-1]
    rows = x_ref.shape[0]
    own_ref[:rows, :] = x_ref[...]
    own_ref[rows:, :] = jnp.concatenate(halves(refs), axis=0).astype(own_ref.dtype)


def copy_share(which_ref, source, target, sem):
    share = target.shape[0]
    start = pl.multiple_of(which_ref[0] * share, share)
    return pltpu.make_async_copy(source.at[pl.ds(start, share), :], target, sem)


def forward_kernel(after_ref, x_ref, d_ref, out_ref):
    gather_rows((x_ref, d_ref), out_ref)


def tile_copies(pairs, sems, i, tile):
    here = block(i, tile)
    return [
        pltpu.make_async_copy(source.at[here, :], target.at[here, :], sems.at[i, k])
        for k, (source, target) in enumerate(pairs)
    ]


def over_tiles(pairs, sems, steps, tile, work):
    for i in range(steps):
        for copy in tile_copies(pairs, sems, i, tile):
            copy.start()

    def step(i, carry):
        def arrived():
            for copy in tile_copies(pairs, sems, i, tile):
                copy.wait()

        work(i, arrived)
        return carry

    lax.fori_loop(0, steps, step, 0)


def own_first_kernel(rows_ref, first_src, hidden_ref, slope_ref, first_ref, sems):
    steps, tile = hidden_ref.shape[0], hidden_ref.shape[2]

    def work(i, arrived):
        arrived()
        hidden, slope = gelu_and_slope(dot_nt(rows_ref[...], first_ref[block(i, tile), :]))
        hidden_ref[i] = hidden
        slope_ref[i] = slope.astype(slope_ref.dtype)

    over_tiles([(first_src, first_ref)], sems, steps, tile, work)


def own_second_kernel(
    cap_rows,
    me_ref,
    own_ref,
    hidden_ref,
    slope_ref,
    second_ref,
    first_ref,
    out_ref,
    total_ref,
    gate_ref,
    held_ref,
    out_sems,
):
    steps, tile = hidden_ref.shape[0], hidden_ref.shape[2]
    rows = total_ref.shape[0]

    def step(j, carry):
        here = block(j, tile)
        back = dot_nt(own_ref[rows:, :], second_ref[here, :])
        terms = hidden_ref[j].astype(jnp.float32) * back
        gate = gate_ref[...]
        for i in range(tile // LANES):
            gate = gate + terms[:, i * LANES : (i + 1) * LANES]
        gate_ref[...] = gate
        d_pre = (back * slope_ref[j].astype(jnp.float32)).astype(jnp.bfloat16)
        total_ref[...] += dot_nn(d_pre, first_ref[here, :])
        return carry

    total_ref[...] = jnp.zeros_like(total_ref)
    gate_ref[...] = jnp.zeros_like(gate_ref)
    lax.fori_loop(0, steps, step, 0)

    experts, copies = out_ref.shape[0], []
    gates = jnp.sum(gate_ref[...], axis=1, keepdims=True)
    lane = lax.broadcasted_iota(jnp.int32, (SUBLANES, LANES), 1)
    for k in range(experts):
        start = k * cap_rows
        tail = jnp.zeros((SUBLANES, LANES), jnp.float32)
        for i in range(cap_rows // SUBLANES):
            here = start + i * SUBLANES
            tail = jnp.where(lane == i, gates[here : here + SUBLANES], tail)
        parts = [
            total_ref[start : start + cap_rows, i * LANES : (i + 1) * LANES]
            for i in range(total_ref.shape[1] // LANES)
        ]
        held_ref[k] = jnp.concatenate(parts + [tail], axis=0).astype(held_ref.dtype)
        source = me_ref[0] ^ (2 * (k % (experts // 2)) + k // (experts // 2))
        copies.append(pltpu.make_async_copy(held_ref.at[k], out_ref.at[source], out_sems.at[k]))
        copies[-1].start()
    for copy in copies:
        copy.wait()


def gather_rows(refs, all_ref):
    rows = refs[0].shape[0]
    for i, ref in enumerate(refs):
        all_ref[i * rows : (i + 1) * rows, :] = ref[...]


def block(i, tile=256):
    return pl.ds(pl.multiple_of(i * tile, tile), tile)


def gelu_rows(weights_ref, rows_ref, hidden_ref, slope_ref):
    tile = weights_ref.shape[0] // 2

    def step(i, carry):
        here = block(i, tile)
        hidden, slope = gelu_and_slope(dot_nt(weights_ref[here, :], rows_ref[...]))
        hidden_ref[here, :] = hidden
        slope_ref[here, :] = slope.astype(slope_ref.dtype)
        return carry

    lax.fori_loop(0, 2, step, 0)


def weight_terms(weights_ref, x_ref, d_ref, hidden_ref, slope_ref, finish):
    tile = weights_ref.shape[0] // 2

    def step(i, carry):
        here = block(i, tile)
        back = dot_nt(weights_ref[here, :], d_ref[...])
        d_pre = (back * slope_ref[here, :].astype(jnp.float32)).astype(jnp.bfloat16)
        finish(i, here, dot_nn(d_pre, x_ref[...]), dot_nn(hidden_ref[here, :], d_ref[...]))
        return carry

    lax.fori_loop(0, 2, step, 0)


def near_first_kernel(
    which_ref,
    after_ref,
    own,
    core,
    first_src,
    second_src,
    hidden_ref,
    slope_ref,
    x_ref,
    d_ref,
    first_ref,
    second_ref,
    sems,
):
    rows = x_ref.shape[0] // 2
    upper, lower = pl.ds(0, rows), pl.ds(rows, rows)
    now = [
        copy_share(which_ref, first_src, first_ref, sems.at[0]),
        pltpu.make_async_copy(own.at[upper, :], x_ref.at[upper, :], sems.at[1]),
        pltpu.make_async_copy(core.at[upper, :], x_ref.at[lower, :], sems.at[2]),
    ]
    later = [
        copy_share(which_ref, second_src, second_ref, sems.at[3]),
        pltpu.make_async_copy(own.at[lower, :], d_ref.at[upper, :], sems.at[4]),
        pltpu.make_async_copy(core.at[lower, :], d_ref.at[lower, :], sems.at[5]),
    ]
    for copy in now + later:
        copy.start()
    for copy in now:
        copy.wait()
    gelu_rows(first_ref, x_ref, hidden_ref, slope_ref)
    for copy in later:
        copy.wait()


def near_second_kernel(after_ref, x_ref, d_ref, hidden_ref, slope_ref, second_ref, gin_ref, gout_ref):
    def finish(i, here, gin, gout):
        gin_ref[here, :] = gin
        gout_ref[here, :] = gout

    weight_terms(second_ref, x_ref, d_ref, hidden_ref, slope_ref, finish)


def far_first_kernel(after_ref, x_over, diagonal_ref, first_ref, hidden_ref, slope_ref, x_ref):
    gather_rows((x_over, diagonal_ref.at[: x_over.shape[0]]), x_ref)
    gelu_rows(first_ref, x_ref, hidden_ref, slope_ref)


def far_second_kernel(
    after_ref,
    d_over,
    diagonal_ref,
    x_ref,
    hidden_ref,
    slope_ref,
    second_ref,
    gin_near,
    gout_near,
    gin_out,
    gout_out,
    d_ref,
    gin_ref,
    gout_ref,
    sems,
):
    gather_rows((d_over, diagonal_ref.at[d_over.shape[0] :]), d_ref)
    tile = second_ref.shape[0] // 2

    def copies(i):
        here = block(i, tile)
        return [
            pltpu.make_async_copy(gin_ref.at[here, :], gin_out.at[here, :], sems.at[i, 0]),
            pltpu.make_async_copy(gout_ref.at[here, :], gout_out.at[here, :], sems.at[i, 1]),
        ]

    def finish(i, here, gin, gout):
        gin_ref[here, :] = (gin_near[here, :] + gin).astype(gin_ref.dtype)
        gout_ref[here, :] = (gout_near[here, :] + gout).astype(gout_ref.dtype)
        for copy in copies(i):
            copy.start()

    weight_terms(second_ref, x_ref, d_ref, hidden_ref, slope_ref, finish)
    for i in range(2):
        for copy in copies(i):
            copy.wait()


def unpack_kernel(
    cap_rows, after_ref, back_ref, gate_ref, expert_ref, slot_ref, tok_ref, dgate_ref
):
    experts = back_ref.shape[0]
    blocks = tok_ref.shape[1] // LANES
    lane = lax.broadcasted_iota(jnp.int32, (SUBLANES, LANES), 1)
    rows, gates = [], []
    for e in range(experts):
        value = back_ref[e].astype(jnp.float32)
        pieces = [value[i * cap_rows : (i + 1) * cap_rows] for i in range(blocks)]
        rows.append(jnp.concatenate(pieces, axis=1))
        tail = value[cap_rows * blocks :]
        gates += [jnp.where(lane == i, tail, 0.0) for i in range(cap_rows // SUBLANES)]
    rows = jnp.concatenate(rows, axis=0).astype(jnp.bfloat16)
    gates = jnp.concatenate(gates, axis=0).astype(jnp.bfloat16)
    chosen = owner_table(expert_ref[...], slot_ref[...], cap_rows, experts * cap_rows)
    table = chosen.astype(jnp.bfloat16)
    tok_ref[...] = dot_tn(table, rows).astype(jnp.bfloat16)
    picked = jnp.sum(dot_tn(gates, table), axis=0, keepdims=True)
    dgate_ref[...] = picked / gate_ref[...]


def in_hbm(*arrays):
    return [pltpu.with_memory_space_constraint(a, pltpu.HBM) for a in arrays]


def body(tokens, upstream, gate_prob, expert_id, slot_index, segment_id, weight_in, weight_out):
    experts = lax.axis_size("expert")
    groups = lax.axis_size("dp")
    tok_rows, width = tokens.shape
    hidden_units = weight_in.shape[1]
    capacity = 5 * tok_rows // (4 * experts)
    cap_rows = -(-capacity // SUBLANES) * SUBLANES
    slots = experts * cap_rows
    share = hidden_units // groups
    gate_row = gate_prob.reshape(1, tok_rows)
    expert_row = expert_id.reshape(1, tok_rows)
    slot_row = slot_index.reshape(1, tok_rows)
    pairs = experts // 2
    which = lax.axis_index("dp").astype(jnp.int32).reshape(1)
    me = lax.axis_index("expert").astype(jnp.int32).reshape(1)
    bf16 = jnp.bfloat16
    anywhere = pl.BlockSpec(memory_space=pl.ANY)
    smem = pl.BlockSpec(memory_space=pltpu.SMEM)
    vmem = pl.BlockSpec(memory_space=pltpu.VMEM)

    unit = 2 * slots * width * hidden_units

    def call(kernel, name, ins, outs, scratch=(), out_spec=vmem, limit=10, work=0.0):
        return pl.pallas_call(
            kernel,
            in_specs=ins,
            out_specs=[out_spec] * len(outs),
            out_shape=[jax.ShapeDtypeStruct(shape, dtype) for shape, dtype in outs],
            scratch_shapes=list(scratch),
            compiler_params=pltpu.CompilerParams(vmem_limit_bytes=limit * MIB),
            cost_estimate=pl.CostEstimate(
                flops=int(work * unit), bytes_accessed=int(work * unit) // 512, transcendentals=0
            ),
            name=name,
        )

    def across(chunk, mask):
        return lax.ppermute(chunk, "expert", [(i, i ^ mask) for i in range(experts)])

    def over(chunk, mask):
        return lax.ppermute(chunk, "dp", [(i, i ^ mask) for i in range(groups)])

    row = (1, tok_rows)
    part = ((2 * cap_rows, width), bf16)
    half = ((pairs * cap_rows, width), bf16)
    *x_parts, d_keep, d_cross = call(
        partial(pack_kernel, cap_rows, experts),
        "pack",
        [smem] + [anywhere] * 6,
        [part] * pairs + [half] * 2,
        [
            pltpu.VMEM((tok_rows, width), bf16),
            pltpu.VMEM((tok_rows, width), bf16),
            pltpu.VMEM(row, jnp.float32),
            pltpu.VMEM(row, jnp.int32),
            pltpu.VMEM(row, jnp.int32),
            pltpu.VMEM(row, jnp.int32),
            pltpu.SemaphoreType.DMA((6,)),
        ],
    )(me, *in_hbm(tokens, upstream, gate_row, expert_row, slot_row, segment_id))
    order = list(range(pairs - 1, 0, -1))
    x_near = {s: across(x_parts[s], 2 * s) for s in order}
    x_near = [x_parts[0]] + [x_near[s] for s in range(1, pairs)]
    d_near = across(d_cross, 1)
    d_parts = call(
        partial(turn_d_kernel, pairs),
        "turn_d",
        [vmem] * 2,
        [part] * pairs,
    )(d_keep, d_near)
    x_keep, x_cross = call(
        turn_x_kernel,
        "turn_x",
        [anywhere] + [vmem] * pairs,
        [half] * 2,
    )(d_parts[0], *x_near)
    d_far = {s: across(d_parts[s], 2 * s) for s in order}
    d_far = [d_parts[0]] + [d_far[s] for s in range(1, pairs)]
    x_own = jnp.concatenate([x_keep, across(x_cross, 1)], axis=0)

    steps = hidden_units // 1024
    wide = ((steps, slots, 1024), bf16)
    weights = pltpu.VMEM((hidden_units, width), bf16)
    hidden, slope = call(
        own_first_kernel,
        "own_first",
        [vmem, anywhere],
        [wide] * 2,
        [weights, pltpu.SemaphoreType.DMA((steps, 1))],
        limit=11,
        work=1,
    )(x_own, *in_hbm(weight_in[0]))
    pair_rows = ((2 * slots, width), bf16)
    (own,) = call(
        join_kernel,
        "join",
        [anywhere] + [vmem] * (pairs + 1),
        [pair_rows],
    )(hidden, x_own, *d_far)
    x_over, d_over, core = over(x_own, 2), over(own[slots:], 2), over(own, 1)

    stride = cap_rows * width // LANES + SUBLANES
    (back,) = call(
        partial(own_second_kernel, cap_rows),
        "own_second",
        [smem] + [vmem] * 5,
        [((experts, stride, LANES), bf16)],
        [
            pltpu.VMEM((slots, width), jnp.float32),
            pltpu.VMEM((slots, LANES), jnp.float32),
            pltpu.VMEM((experts, stride, LANES), bf16),
            pltpu.SemaphoreType.DMA((experts,)),
        ],
        out_spec=anywhere,
        limit=10,
        work=20,
    )(me, own, hidden, slope, weight_out[0], weight_in[0])
    returned = lax.all_to_all(back, "expert", split_axis=0, concat_axis=0, tiled=True)

    wide = ((share, 2 * slots), bf16)
    share_rows = ((share, width), bf16)
    term = ((share, width), jnp.float32)
    hidden_t, slope_t, x_near, d_near, first_share, second_share = call(
        near_first_kernel,
        "near_first",
        [smem] + [anywhere] * 5,
        [wide, wide, pair_rows, pair_rows, share_rows, share_rows],
        [pltpu.SemaphoreType.DMA((6,))],
        work=0.5,
    )(which, back, own, core, *in_hbm(weight_in[0], weight_out[0]))
    gin_near, gout_near = call(
        near_second_kernel,
        "near_second",
        [anywhere] + [vmem] * 5,
        [term, term],
        work=15,
    )(back, x_near, d_near, hidden_t, slope_t, second_share)
    (moved,) = call(
        forward_kernel,
        "forward",
        [anywhere, vmem, vmem],
        [pair_rows],
    )(hidden_t, x_over, d_over)
    diagonal = over(moved, 1)
    hidden_t, slope_t, x_far = call(
        far_first_kernel,
        "far_first",
        [anywhere] + [vmem] * 3,
        [wide, wide, pair_rows],
    )(gin_near, x_over, diagonal, first_share)
    share_block = pltpu.VMEM((share, width), bf16)
    grad_first, grad_second = call(
        far_second_kernel,
        "far_second",
        [anywhere] + [vmem] * 8,
        [share_rows] * 2,
        [pltpu.VMEM(*pair_rows), share_block, share_block, pltpu.SemaphoreType.DMA((2, 2))],
        out_spec=anywhere,
        limit=20,
    )(hidden_t, d_over, diagonal, x_far, hidden_t, slope_t, second_share, gin_near, gout_near)

    d_tokens, d_gate = call(
        partial(unpack_kernel, cap_rows),
        "unpack",
        [anywhere] + [vmem] * 4,
        [((tok_rows, width), bf16), (row, jnp.float32)],
    )(*in_hbm(grad_first), returned, gate_row, expert_row, slot_row)
    return (d_tokens, d_gate.reshape(tok_rows), grad_first[None], grad_second[None])


def solution(mesh):
    in_specs = (
        P(("dp", "expert"), None),
        P(("dp", "expert"), None),
        P(("dp", "expert")),
        P(("dp", "expert")),
        P(("dp", "expert")),
        P(("dp", "expert"), None),
        P("expert", None, None),
        P("expert", None, None),
    )
    out_specs = (
        P(("dp", "expert"), None),
        P(("dp", "expert")),
        P("expert", "dp", None),
        P("expert", "dp", None),
    )
    return jax.shard_map(body, mesh=mesh, in_specs=in_specs, out_specs=out_specs, check_vma=False)
```

```python
from functools import partial

import jax
import jax.numpy as jnp
from jax import lax
from jax.experimental import pallas as pl
from jax.experimental.pallas import tpu as pltpu
from jax.sharding import PartitionSpec as P

SEGS = 4
LANES = 128
SUBLANES = 8
MIB = 1024 * 1024
ROOT_2_PI = 0.7978845608028654
CUBIC = 0.044715


def dot_nn(a, b):
    return lax.dot_general(a, b, (((1,), (0,)), ((), ())), preferred_element_type=jnp.float32)


def dot_nt(a, b):
    return lax.dot_general(a, b, (((1,), (1,)), ((), ())), preferred_element_type=jnp.float32)


def dot_tn(a, b):
    return lax.dot_general(a, b, (((0,), (0,)), ((), ())), preferred_element_type=jnp.float32)


def gelu_and_slope(v):
    square = v * v
    t = jnp.tanh(v * (ROOT_2_PI + (ROOT_2_PI * CUBIC) * square))
    half = 0.5 + 0.5 * t
    hidden = v * half
    slope = half + hidden * (1.0 - t) * (ROOT_2_PI + (3.0 * ROOT_2_PI * CUBIC) * square)
    return hidden.astype(jnp.bfloat16), slope


def owner_table(chunk, slot, cap_rows, slots):
    place = jnp.where(slot >= 0, chunk * cap_rows + slot, -1)
    rows = lax.broadcasted_iota(jnp.int32, (slots, slot.shape[1]), 0)
    return rows == place


def pack_kernel(cap_rows, experts, me_ref, *refs):
    pairs = experts // 2
    sources, x_refs, (keep_ref, cross_ref) = refs[:6], refs[6 : 6 + pairs], refs[6 + pairs : 8 + pairs]
    scratch, sems = refs[8 + pairs : 14 + pairs], refs[14 + pairs]
    copies = [
        pltpu.make_async_copy(src, dst, sems.at[i])
        for i, (src, dst) in enumerate(zip(sources, scratch))
    ]
    for copy in copies:
        copy.start()
    for copy in copies:
        copy.wait()
    tok_ref, up_ref, gate_ref, expert_ref, slot_ref, seg_ref = scratch
    tok_rows = tok_ref.shape[0]
    slots = experts * cap_rows
    chunk, slot = expert_ref[...] ^ me_ref[0], slot_ref[...]
    table = owner_table(chunk, slot, cap_rows, slots).astype(jnp.bfloat16)
    split_rows(dot_nn(table, tok_ref[...]), x_refs)
    seg = seg_ref[...]
    length = jnp.zeros(seg.shape, jnp.float32)
    for label in range(SEGS):
        member = (seg == label).astype(jnp.float32)
        length = length + member * jnp.sum(member, axis=1, keepdims=True)
    weight = tok_rows / (SEGS * length)
    chosen = owner_table((chunk & 1) * pairs + (chunk >> 1), slot, cap_rows, slots)
    table = chosen.astype(jnp.bfloat16)
    weight_col = jnp.sum(jnp.where(chosen, weight, 0.0), axis=1, keepdims=True)
    gate_col = jnp.sum(jnp.where(chosen, gate_ref[...], 0.0), axis=1, keepdims=True)
    cotangent = (dot_nn(table, up_ref[...]) * weight_col).astype(jnp.bfloat16)
    split_rows(cotangent.astype(jnp.float32) * gate_col, (keep_ref, cross_ref))


def split_rows(value, refs):
    rows = value.shape[0] // len(refs)
    for i, ref in enumerate(refs):
        ref[...] = value[i * rows : (i + 1) * rows].astype(ref.dtype)


def halves(refs):
    values = [ref[...].astype(jnp.float32) for ref in refs]
    half = values[0].shape[0] // 2
    return [jnp.concatenate([v[b * half : (b + 1) * half] for v in values], axis=0) for b in (0, 1)]


def turn_d_kernel(pairs, keep_ref, near_ref, *out_refs):
    both = [ref[...].astype(jnp.float32) for ref in (keep_ref, near_ref)]
    rows = both[0].shape[0] // pairs
    for i, ref in enumerate(out_refs):
        ref[...] = jnp.concatenate([v[i * rows : (i + 1) * rows] for v in both], axis=0).astype(ref.dtype)


def turn_x_kernel(after_ref, *refs):
    for ref, value in zip(refs[-2:], halves(refs[:-2])):
        ref[...] = value.astype(ref.dtype)


def join_kernel(after_ref, x_ref, *refs):
    refs, own_ref = refs[:-1], refs[-1]
    rows = x_ref.shape[0]
    own_ref[:rows, :] = x_ref[...]
    own_ref[rows:, :] = jnp.concatenate(halves(refs), axis=0).astype(own_ref.dtype)


def copy_share(which_ref, source, target, sem):
    share = target.shape[0]
    start = pl.multiple_of(which_ref[0] * share, share)
    return pltpu.make_async_copy(source.at[pl.ds(start, share), :], target, sem)


def forward_kernel(after_ref, x_ref, d_ref, out_ref):
    gather_rows((x_ref, d_ref), out_ref)


def tile_copies(pairs, sems, i, tile):
    here = block(i, tile)
    return [
        pltpu.make_async_copy(source.at[here, :], target.at[here, :], sems.at[i, k])
        for k, (source, target) in enumerate(pairs)
    ]


def over_tiles(pairs, sems, steps, tile, work):
    for i in range(steps):
        for copy in tile_copies(pairs, sems, i, tile):
            copy.start()

    def step(i, carry):
        def arrived():
            for copy in tile_copies(pairs, sems, i, tile):
                copy.wait()

        work(i, arrived)
        return carry

    lax.fori_loop(0, steps, step, 0)


def own_first_kernel(rows_ref, first_src, hidden_ref, slope_ref, first_ref, sems):
    steps, tile = hidden_ref.shape[0], hidden_ref.shape[2]

    def work(i, arrived):
        arrived()
        hidden, slope = gelu_and_slope(dot_nt(rows_ref[...], first_ref[block(i, tile), :]))
        hidden_ref[i] = hidden
        slope_ref[i] = slope.astype(slope_ref.dtype)

    over_tiles([(first_src, first_ref)], sems, steps, tile, work)


def own_second_kernel(
    cap_rows,
    me_ref,
    own_ref,
    hidden_ref,
    slope_ref,
    second_ref,
    first_ref,
    out_ref,
    total_ref,
    gate_ref,
    held_ref,
    out_sems,
):
    steps, tile = hidden_ref.shape[0], hidden_ref.shape[2]
    rows = total_ref.shape[0]

    def step(j, carry):
        here = block(j, tile)
        back = dot_nt(own_ref[rows:, :], second_ref[here, :])
        terms = hidden_ref[j].astype(jnp.float32) * back
        gate = gate_ref[...]
        for i in range(tile // LANES):
            gate = gate + terms[:, i * LANES : (i + 1) * LANES]
        gate_ref[...] = gate
        d_pre = (back * slope_ref[j].astype(jnp.float32)).astype(jnp.bfloat16)
        total_ref[...] += dot_nn(d_pre, first_ref[here, :])
        return carry

    total_ref[...] = jnp.zeros_like(total_ref)
    gate_ref[...] = jnp.zeros_like(gate_ref)
    lax.fori_loop(0, steps, step, 0)

    experts, copies = out_ref.shape[0], []
    gates = jnp.sum(gate_ref[...], axis=1, keepdims=True)
    lane = lax.broadcasted_iota(jnp.int32, (SUBLANES, LANES), 1)
    for k in range(experts):
        start = k * cap_rows
        tail = jnp.zeros((SUBLANES, LANES), jnp.float32)
        for i in range(cap_rows // SUBLANES):
            here = start + i * SUBLANES
            tail = jnp.where(lane == i, gates[here : here + SUBLANES], tail)
        parts = [
            total_ref[start : start + cap_rows, i * LANES : (i + 1) * LANES]
            for i in range(total_ref.shape[1] // LANES)
        ]
        held_ref[k] = jnp.concatenate(parts + [tail], axis=0).astype(held_ref.dtype)
        source = me_ref[0] ^ (2 * (k % (experts // 2)) + k // (experts // 2))
        copies.append(pltpu.make_async_copy(held_ref.at[k], out_ref.at[source], out_sems.at[k]))
        copies[-1].start()
    for copy in copies:
        copy.wait()


def gather_rows(refs, all_ref):
    rows = refs[0].shape[0]
    for i, ref in enumerate(refs):
        all_ref[i * rows : (i + 1) * rows, :] = ref[...]


def block(i, tile=256):
    return pl.ds(pl.multiple_of(i * tile, tile), tile)


def gelu_rows(weights_ref, rows_ref, hidden_ref, slope_ref):
    tile = weights_ref.shape[0] // 2

    def step(i, carry):
        here = block(i, tile)
        hidden, slope = gelu_and_slope(dot_nt(weights_ref[here, :], rows_ref[...]))
        hidden_ref[here, :] = hidden
        slope_ref[here, :] = slope.astype(slope_ref.dtype)
        return carry

    lax.fori_loop(0, 2, step, 0)


def weight_terms(weights_ref, x_ref, d_ref, hidden_ref, slope_ref, finish):
    tile = weights_ref.shape[0] // 2

    def step(i, carry):
        here = block(i, tile)
        back = dot_nt(weights_ref[here, :], d_ref[...])
        d_pre = (back * slope_ref[here, :].astype(jnp.float32)).astype(jnp.bfloat16)
        finish(i, here, dot_nn(d_pre, x_ref[...]), dot_nn(hidden_ref[here, :], d_ref[...]))
        return carry

    lax.fori_loop(0, 2, step, 0)


def near_first_kernel(
    which_ref,
    after_ref,
    own,
    core,
    first_src,
    second_src,
    hidden_ref,
    slope_ref,
    x_ref,
    d_ref,
    first_ref,
    second_ref,
    sems,
):
    rows = x_ref.shape[0] // 2
    upper, lower = pl.ds(0, rows), pl.ds(rows, rows)
    now = [
        copy_share(which_ref, first_src, first_ref, sems.at[0]),
        pltpu.make_async_copy(own.at[upper, :], x_ref.at[upper, :], sems.at[1]),
        pltpu.make_async_copy(core.at[upper, :], x_ref.at[lower, :], sems.at[2]),
    ]
    later = [
        copy_share(which_ref, second_src, second_ref, sems.at[3]),
        pltpu.make_async_copy(own.at[lower, :], d_ref.at[upper, :], sems.at[4]),
        pltpu.make_async_copy(core.at[lower, :], d_ref.at[lower, :], sems.at[5]),
    ]
    for copy in now + later:
        copy.start()
    for copy in now:
        copy.wait()
    gelu_rows(first_ref, x_ref, hidden_ref, slope_ref)
    for copy in later:
        copy.wait()


def near_second_kernel(after_ref, x_ref, d_ref, hidden_ref, slope_ref, second_ref, gin_ref, gout_ref):
    def finish(i, here, gin, gout):
        gin_ref[here, :] = gin
        gout_ref[here, :] = gout

    weight_terms(second_ref, x_ref, d_ref, hidden_ref, slope_ref, finish)


def far_first_kernel(after_ref, x_over, diagonal_ref, first_ref, hidden_ref, slope_ref, x_ref):
    gather_rows((x_over, diagonal_ref.at[: x_over.shape[0]]), x_ref)
    gelu_rows(first_ref, x_ref, hidden_ref, slope_ref)


def far_second_kernel(
    after_ref,
    d_over,
    diagonal_ref,
    x_ref,
    hidden_ref,
    slope_ref,
    second_ref,
    gin_near,
    gout_near,
    gin_out,
    gout_out,
    d_ref,
    gin_ref,
    gout_ref,
    sems,
):
    gather_rows((d_over, diagonal_ref.at[d_over.shape[0] :]), d_ref)
    tile = second_ref.shape[0] // 2

    def copies(i):
        here = block(i, tile)
        return [
            pltpu.make_async_copy(gin_ref.at[here, :], gin_out.at[here, :], sems.at[i, 0]),
            pltpu.make_async_copy(gout_ref.at[here, :], gout_out.at[here, :], sems.at[i, 1]),
        ]

    def finish(i, here, gin, gout):
        gin_ref[here, :] = (gin_near[here, :] + gin).astype(gin_ref.dtype)
        gout_ref[here, :] = (gout_near[here, :] + gout).astype(gout_ref.dtype)
        for copy in copies(i):
            copy.start()

    weight_terms(second_ref, x_ref, d_ref, hidden_ref, slope_ref, finish)
    for i in range(2):
        for copy in copies(i):
            copy.wait()


def unpack_kernel(
    cap_rows, after_ref, back_ref, gate_ref, expert_ref, slot_ref, tok_ref, dgate_ref
):
    experts = back_ref.shape[0]
    blocks = tok_ref.shape[1] // LANES
    lane = lax.broadcasted_iota(jnp.int32, (SUBLANES, LANES), 1)
    rows, gates = [], []
    for e in range(experts):
        value = back_ref[e].astype(jnp.float32)
        pieces = [value[i * cap_rows : (i + 1) * cap_rows] for i in range(blocks)]
        rows.append(jnp.concatenate(pieces, axis=1))
        tail = value[cap_rows * blocks :]
        gates += [jnp.where(lane == i, tail, 0.0) for i in range(cap_rows // SUBLANES)]
    rows = jnp.concatenate(rows, axis=0).astype(jnp.bfloat16)
    gates = jnp.concatenate(gates, axis=0).astype(jnp.bfloat16)
    chosen = owner_table(expert_ref[...], slot_ref[...], cap_rows, experts * cap_rows)
    table = chosen.astype(jnp.bfloat16)
    tok_ref[...] = dot_tn(table, rows).astype(jnp.bfloat16)
    picked = jnp.sum(dot_tn(gates, table), axis=0, keepdims=True)
    dgate_ref[...] = picked / gate_ref[...]


def in_hbm(*arrays):
    return [pltpu.with_memory_space_constraint(a, pltpu.HBM) for a in arrays]


def body(tokens, upstream, gate_prob, expert_id, slot_index, segment_id, weight_in, weight_out):
    experts = lax.axis_size("expert")
    groups = lax.axis_size("dp")
    tok_rows, width = tokens.shape
    hidden_units = weight_in.shape[1]
    capacity = 5 * tok_rows // (4 * experts)
    cap_rows = -(-capacity // SUBLANES) * SUBLANES
    slots = experts * cap_rows
    share = hidden_units // groups
    gate_row = gate_prob.reshape(1, tok_rows)
    expert_row = expert_id.reshape(1, tok_rows)
    slot_row = slot_index.reshape(1, tok_rows)
    pairs = experts // 2
    which = lax.axis_index("dp").astype(jnp.int32).reshape(1)
    me = lax.axis_index("expert").astype(jnp.int32).reshape(1)
    bf16 = jnp.bfloat16
    anywhere = pl.BlockSpec(memory_space=pl.ANY)
    smem = pl.BlockSpec(memory_space=pltpu.SMEM)
    vmem = pl.BlockSpec(memory_space=pltpu.VMEM)

    unit = 2 * slots * width * hidden_units

    def call(kernel, name, ins, outs, scratch=(), out_spec=vmem, limit=10, work=0.0):
        return pl.pallas_call(
            kernel,
            in_specs=ins,
            out_specs=[out_spec] * len(outs),
            out_shape=[jax.ShapeDtypeStruct(shape, dtype) for shape, dtype in outs],
            scratch_shapes=list(scratch),
            compiler_params=pltpu.CompilerParams(vmem_limit_bytes=limit * MIB),
            cost_estimate=pl.CostEstimate(
                flops=int(work * unit), bytes_accessed=int(work * unit) // 512, transcendentals=0
            ),
            name=name,
        )

    def across(chunk, mask):
        return lax.ppermute(chunk, "expert", [(i, i ^ mask) for i in range(experts)])

    def over(chunk, mask):
        return lax.ppermute(chunk, "dp", [(i, i ^ mask) for i in range(groups)])

    row = (1, tok_rows)
    part = ((2 * cap_rows, width), bf16)
    half = ((pairs * cap_rows, width), bf16)
    *x_parts, d_keep, d_cross = call(
        partial(pack_kernel, cap_rows, experts),
        "pack",
        [smem] + [anywhere] * 6,
        [part] * pairs + [half] * 2,
        [
            pltpu.VMEM((tok_rows, width), bf16),
            pltpu.VMEM((tok_rows, width), bf16),
            pltpu.VMEM(row, jnp.float32),
            pltpu.VMEM(row, jnp.int32),
            pltpu.VMEM(row, jnp.int32),
            pltpu.VMEM(row, jnp.int32),
            pltpu.SemaphoreType.DMA((6,)),
        ],
    )(me, *in_hbm(tokens, upstream, gate_row, expert_row, slot_row, segment_id))
    order = list(range(pairs - 1, 0, -1))
    x_near = {s: across(x_parts[s], 2 * s) for s in order}
    x_near = [x_parts[0]] + [x_near[s] for s in range(1, pairs)]
    d_near = across(d_cross, 1)
    d_parts = call(
        partial(turn_d_kernel, pairs),
        "turn_d",
        [vmem] * 2,
        [part] * pairs,
    )(d_keep, d_near)
    x_keep, x_cross = call(
        turn_x_kernel,
        "turn_x",
        [anywhere] + [vmem] * pairs,
        [half] * 2,
    )(d_parts[0], *x_near)
    d_far = {s: across(d_parts[s], 2 * s) for s in order}
    d_far = [d_parts[0]] + [d_far[s] for s in range(1, pairs)]
    x_own = jnp.concatenate([x_keep, across(x_cross, 1)], axis=0)

    steps = hidden_units // 1536
    wide = ((steps, slots, 1536), bf16)
    weights = pltpu.VMEM((hidden_units, width), bf16)
    hidden, slope = call(
        own_first_kernel,
        "own_first",
        [vmem, anywhere],
        [wide] * 2,
        [weights, pltpu.SemaphoreType.DMA((steps, 1))],
        limit=16,
        work=1,
    )(x_own, *in_hbm(weight_in[0]))
    pair_rows = ((2 * slots, width), bf16)
    (own,) = call(
        join_kernel,
        "join",
        [anywhere] + [vmem] * (pairs + 1),
        [pair_rows],
    )(hidden, x_own, *d_far)
    x_over, d_over, core = over(x_own, 2), over(own[slots:], 2), over(own, 1)

    stride = cap_rows * width // LANES + SUBLANES
    (back,) = call(
        partial(own_second_kernel, cap_rows),
        "own_second",
        [smem] + [vmem] * 5,
        [((experts, stride, LANES), bf16)],
        [
            pltpu.VMEM((slots, width), jnp.float32),
            pltpu.VMEM((slots, LANES), jnp.float32),
            pltpu.VMEM((experts, stride, LANES), bf16),
            pltpu.SemaphoreType.DMA((experts,)),
        ],
        out_spec=anywhere,
        limit=16,
        work=20,
    )(me, own, hidden, slope, weight_out[0], weight_in[0])
    returned = lax.all_to_all(back, "expert", split_axis=0, concat_axis=0, tiled=True)

    wide = ((share, 2 * slots), bf16)
    share_rows = ((share, width), bf16)
    term = ((share, width), jnp.float32)
    hidden_t, slope_t, x_near, d_near, first_share, second_share = call(
        near_first_kernel,
        "near_first",
        [smem] + [anywhere] * 5,
        [wide, wide, pair_rows, pair_rows, share_rows, share_rows],
        [pltpu.SemaphoreType.DMA((6,))],
        work=0.5,
    )(which, back, own, core, *in_hbm(weight_in[0], weight_out[0]))
    gin_near, gout_near = call(
        near_second_kernel,
        "near_second",
        [anywhere] + [vmem] * 5,
        [term, term],
        work=15,
    )(back, x_near, d_near, hidden_t, slope_t, second_share)
    (moved,) = call(
        forward_kernel,
        "forward",
        [anywhere, vmem, vmem],
        [pair_rows],
    )(hidden_t, x_over, d_over)
    diagonal = over(moved, 1)
    hidden_t, slope_t, x_far = call(
        far_first_kernel,
        "far_first",
        [anywhere] + [vmem] * 3,
        [wide, wide, pair_rows],
    )(gin_near, x_over, diagonal, first_share)
    share_block = pltpu.VMEM((share, width), bf16)
    grad_first, grad_second = call(
        far_second_kernel,
        "far_second",
        [anywhere] + [vmem] * 8,
        [share_rows] * 2,
        [pltpu.VMEM(*pair_rows), share_block, share_block, pltpu.SemaphoreType.DMA((2, 2))],
        out_spec=anywhere,
        limit=20,
    )(hidden_t, d_over, diagonal, x_far, hidden_t, slope_t, second_share, gin_near, gout_near)

    d_tokens, d_gate = call(
        partial(unpack_kernel, cap_rows),
        "unpack",
        [anywhere] + [vmem] * 4,
        [((tok_rows, width), bf16), (row, jnp.float32)],
    )(*in_hbm(grad_first), returned, gate_row, expert_row, slot_row)
    return (d_tokens, d_gate.reshape(tok_rows), grad_first[None], grad_second[None])


def solution(mesh):
    in_specs = (
        P(("dp", "expert"), None),
        P(("dp", "expert"), None),
        P(("dp", "expert")),
        P(("dp", "expert")),
        P(("dp", "expert")),
        P(("dp", "expert"), None),
        P("expert", None, None),
        P("expert", None, None),
    )
    out_specs = (
        P(("dp", "expert"), None),
        P(("dp", "expert")),
        P("expert", "dp", None),
        P("expert", "dp", None),
    )
    return jax.shard_map(body, mesh=mesh, in_specs=in_specs, out_specs=out_specs, check_vma=False)
```
